256 devices in a mesh: fsdp: 64 (over z, x, core), dp: 4 (over y).
Axes of the slice: x: 4, y: 4, z: 8, core: 2. Of those that a mesh axis runs over, the one named last changes fastest.
Arguments:
- gradient: bfloat16 [8, 1024, 8, 1024], P(None, 'fsdp', None, 'dp'), may hold values from -2 to 2
- second_moment: float32 [8, 1024, 8, 1024], P(None, 'fsdp', None, 'dp'), may hold values from 1e-06 to 0.001
- stat_left: float32 [128, 1024, 1024], P('fsdp', 'dp'), may hold values from -6 to 6
- stat_right: float32 [128, 1024, 1024], P('fsdp', 'dp'), may hold values from -6 to 6
- root_left: bfloat16 [128, 1024, 1024], P('fsdp', 'dp'), may hold values from -0.1875 to 0.1875
- root_right: bfloat16 [128, 1024, 1024], P('fsdp', None, 'dp'), may hold values from -0.1875 to 0.1875
- block_slot: int32 [64], replicated, may hold values from 0 to 127, as said below
Outputs:
- new_left: float32 [128, 1024, 1024], P('fsdp', 'dp')
- new_right: float32 [128, 1024, 1024], P('fsdp', 'dp')
- new_second: float32 [8, 1024, 8, 1024], P(None, 'fsdp', None, 'dp')
- direction: bfloat16 [8, 1024, 8, 1024], P(None, 'fsdp', None, 'dp')
The draws below stay inside these ranges and needn't reach their ends.
Inputs may be any that keep to these rules, and one draw needn't show every extreme that they name: `block_slot`: all entries differ; slot s belongs to owner s // 2; some owner holds 2 blocks.
All inputs are finite; a program needn't handle non-finite values.
Results may differ from the reference program's by a relative error of at most 0.0058.
Values may be sent and summed in bfloat16 or wider, within the bound.
No kernel may reach another device: no remote copies, remote signals or barrier semaphores. Data moves between devices by JAX's collectives and lax.ppermute only.
A program may use at most 64 MiB of HBM per device.

```python
import math
import jax
import jax.numpy as jnp
from jax import lax

BLK = 1024
COLBLK = 8
RB = 8
BLOCKS = 64
SLOTS = 2
SLOT_ALL = 128


def draw_gradient(key, part):
    key = jax.random.fold_in(key, 11)
    first_key, second_key = jax.random.split(key)
    positions = jnp.arange(BLK, dtype=jnp.float32) / (BLK - 1)
    column_scale = jnp.exp(jax.random.uniform(second_key, (COLBLK, BLK), jnp.float32) * math.log(4.0))
    row_scale = jnp.exp(positions * math.log(10.0))
    values = jnp.clip(jax.random.normal(first_key, (RB, BLK, COLBLK, BLK), jnp.float32), -6.0, 6.0)
    values = 0.005 * values * row_scale[None, :, None, None] * column_scale[None, None, :, :]
    return values.astype(jnp.bfloat16)


def draw_block_slot(key, part):
    key = jax.random.fold_in(key, 23)
    owner_key, score_key, order_key = jax.random.split(key, 3)
    full_owner = jax.random.randint(owner_key, (), 0, SLOT_ALL // SLOTS)
    scores = jax.random.permutation(score_key, SLOT_ALL).astype(jnp.int32)
    owners = jnp.arange(SLOT_ALL, dtype=jnp.int32) // SLOTS
    scores = scores - jnp.where(owners == full_owner, SLOT_ALL, 0).astype(jnp.int32)
    ordered = jnp.argsort(scores, stable=True).astype(jnp.int32)
    chosen = ordered[:BLOCKS]
    shuffled = jax.random.permutation(order_key, BLOCKS).astype(jnp.int32)
    result = jnp.zeros((BLOCKS,), jnp.int32).at[shuffled].set(chosen)
    return result


def shard_levels(own_key, extent, cuts, smallest, high):
    def one(position, blocks):
        draws = jax.random.uniform(jax.random.fold_in(jax.random.fold_in(own_key, 6), position), (blocks,), jnp.float32, smallest / len(cuts), high / len(cuts))
        return jnp.repeat(jnp.exp(draws), extent[position] // blocks).reshape((-1,) + (1,) * (len(extent) - position - 1))

    level = one(*cuts[0])
    for cut in cuts[1:]:
        level = level * one(*cut)
    return level


def normal_values(stream_key, dims, deviation, bound, pieces=(), held_as=jnp.bfloat16):
    array = jax.random.normal(stream_key, dims, jnp.float32) * deviation
    if len(pieces) > 0:
        array = shard_levels(stream_key, dims, pieces, -0.22, 0.18) * array
    return jnp.clip(array, min=-bound, max=bound).astype(held_as)


def setup_inputs(seed: int = 0) -> dict:
    key_of = jax.random.split(jax.random.key(seed), 8)
    gradient = draw_gradient(jax.random.fold_in(key_of[7], 71), 0)
    second_moment = jnp.clip(jnp.exp(math.log(0.001) - 6.9077553 * jax.random.uniform(key_of[1], (RB, BLK, COLBLK, BLK), jnp.float32) ** shard_levels(key_of[1], (RB, BLK, COLBLK, BLK), ((1, 64), (3, 4)), -0.2, 0.2)), 9.999999974752427e-07, 0.001)
    stat_left = normal_values(key_of[2], (SLOT_ALL, BLK, BLK), 1.0, 6.0, ((0, 64), (1, 4)), jnp.float32)
    stat_right = normal_values(key_of[3], (SLOT_ALL, BLK, BLK), 1.0, 6.0, ((0, 64), (1, 4)), jnp.float32)
    root_left = normal_values(key_of[4], (SLOT_ALL, BLK, BLK), BLK ** -0.5, 0.1875, ((0, 64), (1, 4)))
    root_right = normal_values(key_of[5], (SLOT_ALL, BLK, BLK), BLK ** -0.5, 0.1875, ((0, 64), (2, 4)))
    block_slot = draw_block_slot(jax.random.fold_in(key_of[7], 71), 0)
    return dict(gradient=gradient, second_moment=second_moment, stat_left=stat_left, stat_right=stat_right, root_left=root_left, root_right=root_right, block_slot=block_slot)


def reference(gradient, second_moment, stat_left, stat_right, root_left, root_right, block_slot):
    grad_blocks = gradient.transpose(0, 2, 1, 3).reshape(BLOCKS, BLK, BLK)
    slot_block = jnp.full((SLOT_ALL,), -1, jnp.int32).at[block_slot].set(jnp.arange(BLOCKS, dtype=jnp.int32))

    def per_slot(items):
        left_stat, right_stat, left_root, right_root, slot_entry = items
        grad_block = lax.dynamic_index_in_dim(grad_blocks, jnp.maximum(slot_entry, 0).astype(jnp.int32), 0, keepdims=False)
        grad_block = jnp.where(slot_entry >= 0, grad_block, jnp.zeros_like(grad_block))
        left_next = left_stat + jnp.dot(grad_block, grad_block.T, preferred_element_type=jnp.float32)
        right_next = right_stat + jnp.dot(grad_block.T, grad_block, preferred_element_type=jnp.float32)
        mixed = jnp.dot(grad_block, right_root, preferred_element_type=jnp.float32).astype(jnp.bfloat16)
        update = jnp.dot(left_root, mixed, preferred_element_type=jnp.float32).astype(jnp.bfloat16)
        return (left_next, right_next, update)
    new_left, new_right, updates = lax.map(per_slot, (stat_left, stat_right, root_left, root_right, slot_block))
    update_values = updates[block_slot].astype(jnp.float32)
    update_norm = lax.optimization_barrier(jnp.sum(update_values * update_values, axis=(1, 2)))
    grad_values = gradient.astype(jnp.float32)
    new_second = 0.9 * second_moment + 0.1 * grad_values * grad_values
    adam = grad_values / (jnp.sqrt(new_second) + 1e-08)
    adam_norm = lax.optimization_barrier(jnp.sum(adam * adam, axis=(1, 3))).reshape(BLOCKS)
    scaling = jnp.sqrt(adam_norm / (update_norm + 1e-06))
    scaled = (scaling[:, None, None] * update_values).astype(jnp.bfloat16)
    direction = scaled.reshape(RB, COLBLK, BLK, BLK).transpose(0, 2, 1, 3)
    return (new_left, new_right, new_second, direction)
```

```python
import jax
import jax.numpy as jnp
from jax import lax
from jax.experimental import pallas as pl
from jax.experimental.pallas import tpu as pltpu
from jax.sharding import PartitionSpec as P

AXES = ("fsdp", "dp")
F32 = jnp.float32
BF16 = jnp.bfloat16
SMEM = pl.BlockSpec(memory_space=pltpu.SMEM)
VMEM = pl.BlockSpec(memory_space=pltpu.VMEM)
MIB = 1 << 20


def local(kernel, outs, inputs, scratch=(), limit=16, flops=0, moved=0):
    return pl.pallas_call(
        kernel,
        out_shape=outs,
        in_specs=[SMEM] + [VMEM] * (len(inputs) - 1),
        out_specs=jax.tree.map(lambda _: VMEM, outs),
        scratch_shapes=list(scratch),
        compiler_params=pltpu.CompilerParams(vmem_limit_bytes=limit * MIB),
        cost_estimate=pl.CostEstimate(flops=flops, bytes_accessed=moved, transcendentals=0),
    )(*inputs)


def shape(dims, dtype):
    return jax.ShapeDtypeStruct(dims, dtype)


def spread_row(slot):
    return ((slot >> 2) << 3) + (slot & 3)


def spread_kernel(slot_ref, grad_ref, after_ref, out_ref, wide):
    row_blocks, rows, column_blocks, quarter = grad_ref.shape
    half = quarter // 2
    out_ref[...] = jnp.zeros_like(out_ref)
    size = wide.shape[0] // 2
    for h in range(2):
        wide[h * size : (h + 1) * size, :] = grad_ref[..., h * half : (h + 1) * half].astype(F32).reshape(size, half)
    for b in range(row_blocks * column_blocks):
        start = (b // column_blocks) * rows * column_blocks + b % column_blocks
        at = spread_row(slot_ref[b])
        out_ref[at] = wide[pl.ds(start, rows, stride=column_blocks), :].astype(BF16)
        out_ref[at + 4] = wide[pl.ds(size + start, rows, stride=column_blocks), :].astype(BF16)


def moment_kernel(slot_ref, grad_ref, second_ref, new_ref, sent_ref, part):
    row_blocks, _, column_blocks, _ = grad_ref.shape
    sent_ref[...] = jnp.zeros_like(sent_ref)
    for r in range(row_blocks):
        g = grad_ref[r].astype(F32)
        new = 0.9 * second_ref[r] + 0.1 * g * g
        new_ref[r] = new
        adam = g / (jnp.sqrt(new) + 1e-08)
        sums = jnp.sum(jnp.sum(adam * adam, axis=0), axis=1, keepdims=True)
        part[r * column_blocks : (r + 1) * column_blocks, :] = jnp.broadcast_to(sums, (column_blocks, 128))
    for b in range(row_blocks * column_blocks):
        at = spread_row(slot_ref[b])
        sent_ref[at] = part[b : b + 1, :]
        sent_ref[at + 4] = part[b : b + 1, :]


def pack_kernel(spot_ref, left_ref, right_ref, *outs):
    half = left_ref.shape[1] // 2
    chips = len(outs) // 2
    for m in range(chips):
        to = spot_ref[0] ^ m
        part = pl.ds(pl.multiple_of((to >> 1) * half, half), half)
        outs[m][...] = left_ref[to & 1, part, :]
        outs[chips + m][...] = right_ref[to & 1, :, part]


def update_kernel(spot_ref, adam_ref, own_ref, other_ref, *refs):
    lefts, lefts2, rights = refs[0:4], refs[4:8], refs[8:12]
    grad, update_ref, norm_ref, note_ref, root, mixed, rows = refs[12:]
    core, lane = spot_ref[1], spot_ref[2]
    owners, chips, piece, half = own_ref.shape
    order = grad.shape[0]
    for d in range(chips):
        mine = pl.multiple_of((2 * d + core) * half, half)
        theirs = pl.multiple_of((2 * d + 1 - core) * half, half)
        grad[:, pl.ds(mine, half)] = own_ref[:, d].reshape(order, half)
        grad[:, pl.ds(theirs, half)] = other_ref[:, d].reshape(order, half)
        root[:, pl.ds(pl.multiple_of((lane ^ d) * half, half), half)] = rights[d][...]
    for t in range(0, order, 512):
        mixed[t : t + 512, :] = jnp.dot(grad[t : t + 512, :], root[...], preferred_element_type=F32).astype(BF16)
    total = jnp.zeros((8, 128), F32)
    count = half // piece
    for parts, which, first in ((lefts, core, lane), (lefts2, 1 - core, lane ^ 2)):
        for m in range(chips):
            rows[m * half : (m + 1) * half, :] = parts[m][...]
        part = jnp.dot(rows[...], mixed[...], preferred_element_type=F32).astype(BF16)
        wide = part.astype(F32)
        squares = jnp.sum((wide * wide).reshape(chips * half // 8, 8, chips * half), axis=0)
        for y in range(chips):
            total = total + squares[:, y * half : (y + 1) * half]
            for m in range(chips):
                block = part[m * half : (m + 1) * half, y * half : (y + 1) * half]
                spot = (first ^ m) * (2 * count) + which * count
                update_ref[pl.ds(spot, count), y] = block.reshape(count, piece, half)
    norm = jnp.sum(jnp.sum(total, axis=0, keepdims=True), axis=1, keepdims=True)
    norm_ref[...] = jnp.broadcast_to(norm, norm_ref.shape)
    note_ref[...] = jnp.broadcast_to(jnp.sum(adam_ref[...], axis=0), note_ref.shape)


def product_kernel(spot_ref, grad, *refs):
    outs, (rows, columns) = refs[:-2], refs[-2:]
    core, lane = spot_ref[1], spot_ref[2]
    order = grad.shape[0]
    half = rows.shape[0] // 4
    for m in range(4):
        d = lane ^ m
        rows[m * half : (m + 1) * half, :] = grad[pl.ds(pl.multiple_of(d * 2 * half + core * half, half), half), :]
        columns[m * half : (m + 1) * half, :] = grad[:, pl.ds(pl.multiple_of((2 * d + core) * half, half), half)].T
    for n in range(0, order, 256):
        left = lax.dot_general(rows[...], grad[n : n + 256, :], (((1,), (1,)), ((), ())), preferred_element_type=F32)
        right = jnp.dot(columns[...], grad[:, n : n + 256], preferred_element_type=F32)
        for m, out in enumerate(outs):
            out[:half, n : n + 256] = left[m * half : (m + 1) * half].astype(BF16)
            out[half:, n : n + 256] = right[m * half : (m + 1) * half].astype(BF16)


def graft_kernel(spot_ref, update_ref, norm_ref, norm2_ref, note_ref, after_ref, out_ref):
    scale = jnp.sqrt(note_ref[0:1, :] / (norm_ref[0:1, :] + norm2_ref[0:1, :] + 1e-06))
    out_ref[...] = (update_ref[...].astype(F32) * scale[None, None]).astype(BF16)


def stat_kernel(spot_ref, p0, p1, p2, p3, left_ref, right_ref, new_left_ref, new_right_ref):
    half = left_ref.shape[1]
    for m, ref in enumerate((p0, p1, p2, p3)):

        @pl.when(pl.program_id(0) == m)
        def _():
            new_left_ref[0] = left_ref[0] + ref[:half, :].astype(F32)
            new_right_ref[0] = right_ref[0] + ref[half:, :].astype(F32)


def direction_kernel(slot_ref, values_ref, out_ref, wide):
    row_blocks, rows, column_blocks, quarter = out_ref.shape
    half = quarter // 2
    size = wide.shape[0] // 2
    for b in range(row_blocks * column_blocks):
        at = spread_row(slot_ref[b])
        start = (b // column_blocks) * rows * column_blocks + b % column_blocks
        wide[pl.ds(start, rows, stride=column_blocks), :] = values_ref[at].astype(F32)
        wide[pl.ds(size + start, rows, stride=column_blocks), :] = values_ref[at + 4].astype(F32)
    for h in range(2):
        part = wide[h * size : (h + 1) * size, :].reshape(row_blocks, rows, column_blocks, half)
        out_ref[..., h * half : (h + 1) * half] = part.astype(out_ref.dtype)


def body(gradient, second_moment, stat_left, stat_right, root_left, root_right, block_slot):
    owners = lax.axis_size("fsdp")
    chips = lax.axis_size("dp")
    devices = owners * chips
    row_blocks, piece_rows, column_blocks, quarter = gradient.shape
    blocks = row_blocks * column_blocks
    order = stat_left.shape[2]
    half = quarter // 2
    core = lax.axis_index("fsdp") % 2
    chip = lax.axis_index("dp")
    spot = jnp.stack([chip, core, 2 * core + chip % 2]).astype(jnp.int32)

    def matching(m, back):
        pairs = []
        for k in range(owners // 2):
            for c in range(2):
                for d in range(chips):
                    c2, j = (d ^ m) >> 1, (d ^ m) & 1
                    here = (2 * k + c) * chips + d
                    there = (2 * k + c2) * chips + 2 * c + j
                    pairs.append((there, here) if back else (here, there))
        return pairs

    swap = [(i, i ^ 1) for i in range(owners)]

    packed = local(
        pack_kernel,
        [shape((half, order), BF16)] * chips + [shape((order, half), BF16)] * chips,
        (spot, root_left, root_right),
        moved=4 * MIB,
    )
    lefts = [lax.ppermute(packed[m], AXES, matching(m, False)) for m in range(chips)]
    rights = [lax.ppermute(packed[chips + m], AXES, matching(m, False)) for m in range(chips)]

    pieces = local(
        spread_kernel, shape((devices, piece_rows, half), BF16), (block_slot, gradient, packed[0]),
        scratch=[pltpu.VMEM((2 * blocks * piece_rows, half), F32)], moved=MIB * 3 // 2,
    )
    own = lax.all_to_all(pieces, AXES, split_axis=0, concat_axis=0, tiled=True)

    new_second, sent = local(
        moment_kernel,
        [shape(second_moment.shape, F32), shape((devices, 1, 128), F32)],
        (block_slot, gradient, second_moment),
        scratch=[pltpu.VMEM((blocks, 128), F32)], moved=MIB * 5 // 2,
    )
    adam = lax.all_to_all(sent, AXES, split_axis=0, concat_axis=0, tiled=True)

    own, adam = lax.optimization_barrier((own, adam))
    lefts2 = [lax.ppermute(part, "fsdp", swap) for part in lefts]
    other = lax.ppermute(own, "fsdp", swap)

    cut = (owners, chips, piece_rows, half)
    grad, update, norm, note = local(
        update_kernel,
        [shape((order, order), BF16), shape(cut, BF16), shape((8, 128), F32), shape((8, 128), F32)],
        (spot, adam, own.reshape(cut), other.reshape(cut), *lefts, *lefts2, *rights),
        scratch=[
            pltpu.VMEM((order, order // 2), BF16), pltpu.VMEM((order, order // 2), BF16),
            pltpu.VMEM((order // 2, order), BF16),
        ],
        limit=32, flops=2 * order * order * order, moved=8 * MIB,
    )
    norm2 = lax.ppermute(norm, "fsdp", swap)
    products = local(
        product_kernel, [shape((2 * half, order), BF16)] * chips, (spot, grad),
        scratch=[pltpu.VMEM((order // 2, order), BF16)] * 2,
        limit=24, flops=2 * order * order * order, moved=4 * MIB,
    )
    back = local(graft_kernel, shape(cut, BF16), (spot, update, norm, norm2, note, products[0]), moved=2 * MIB)
    products = [lax.ppermute(products[m], AXES, matching(m, True)) for m in range(chips)]
    returned = lax.all_to_all(back.reshape(devices, piece_rows, half), AXES, split_axis=0, concat_axis=0, tiled=True)

    whole = pl.BlockSpec((2 * half, order), lambda m, s: (0, 0))
    piece = pl.BlockSpec((1, half, order), lambda m, s: ((s[0] ^ m) & 1, (s[0] ^ m) >> 1, 0))
    new_left, new_right = pl.pallas_call(
        stat_kernel,
        out_shape=[shape(stat_left.shape, F32), shape(stat_right.shape, F32)],
        grid_spec=pltpu.PrefetchScalarGridSpec(
            num_scalar_prefetch=1, grid=(chips,), in_specs=[whole] * chips + [piece] * 2, out_specs=[piece] * 2
        ),
        compiler_params=pltpu.CompilerParams(vmem_limit_bytes=16 * MIB),
        cost_estimate=pl.CostEstimate(flops=0, bytes_accessed=10 * MIB, transcendentals=0),
    )(spot, *products, stat_left, stat_right)

    direction = local(
        direction_kernel, shape(gradient.shape, gradient.dtype), (block_slot, returned),
        scratch=[pltpu.VMEM((2 * blocks * piece_rows, half), F32)],
        moved=2 * MIB,
    )
    return (new_left, new_right, new_second, direction)


def solution(mesh):
    placed = (
        P(None, "fsdp", None, "dp"),
        P(None, "fsdp", None, "dp"),
        P("fsdp", "dp", None),
        P("fsdp", "dp", None),
        P("fsdp", "dp", None),
        P("fsdp", None, "dp"),
        P(),
    )
    return jax.shard_map(
        body,
        mesh=mesh,
        in_specs=placed,
        out_specs=(
            P("fsdp", "dp", None),
            P("fsdp", "dp", None),
            P(None, "fsdp", None, "dp"),
            P(None, "fsdp", None, "dp"),
        ),
        check_vma=False,
    )
```

```python
import jax
import jax.numpy as jnp
from jax import lax
from jax.experimental import pallas as pl
from jax.experimental.pallas import tpu as pltpu
from jax.sharding import PartitionSpec as P

AXES = ("fsdp", "dp")
F32 = jnp.float32
BF16 = jnp.bfloat16
SMEM = pl.BlockSpec(memory_space=pltpu.SMEM)
VMEM = pl.BlockSpec(memory_space=pltpu.VMEM)
MIB = 1 << 20


def local(kernel, outs, inputs, scratch=(), limit=16, flops=0, moved=0):
    return pl.pallas_call(
        kernel,
        out_shape=outs,
        in_specs=[SMEM] + [VMEM] * (len(inputs) - 1),
        out_specs=jax.tree.map(lambda _: VMEM, outs),
        scratch_shapes=list(scratch),
        compiler_params=pltpu.CompilerParams(vmem_limit_bytes=limit * MIB),
        cost_estimate=pl.CostEstimate(flops=flops, bytes_accessed=moved, transcendentals=0),
    )(*inputs)


def shape(dims, dtype):
    return jax.ShapeDtypeStruct(dims, dtype)


def spread_row(slot):
    return ((slot >> 2) << 3) + (slot & 3)


def spread_kernel(slot_ref, grad_ref, after_ref, out_ref, wide):
    row_blocks, rows, column_blocks, quarter = grad_ref.shape
    half = quarter // 2
    out_ref[...] = jnp.zeros_like(out_ref)
    size = wide.shape[0] // 2
    for h in range(2):
        wide[h * size : (h + 1) * size, :] = grad_ref[..., h * half : (h + 1) * half].astype(F32).reshape(size, half)
    for b in range(row_blocks * column_blocks):
        start = (b // column_blocks) * rows * column_blocks + b % column_blocks
        at = spread_row(slot_ref[b])
        out_ref[at] = wide[pl.ds(start, rows, stride=column_blocks), :].astype(BF16)
        out_ref[at + 4] = wide[pl.ds(size + start, rows, stride=column_blocks), :].astype(BF16)


def moment_kernel(slot_ref, grad_ref, second_ref, new_ref, sent_ref, part):
    row_blocks, _, column_blocks, _ = grad_ref.shape
    part[...] = jnp.zeros_like(part)
    for r in range(row_blocks):
        g = grad_ref[r].astype(F32)
        new = 0.9 * second_ref[r] + 0.1 * g * g
        new_ref[r] = new
        adam = g / (jnp.sqrt(new) + 1e-08)
        sums = jnp.sum(jnp.sum(adam * adam, axis=0), axis=1, keepdims=True)
        part[r * column_blocks : (r + 1) * column_blocks, :] = jnp.broadcast_to(sums, (column_blocks, 128))
    sent_ref[...] = part[...].T[0:8, :]


def pack_kernel(spot_ref, left_ref, right_ref, *outs):
    half = left_ref.shape[1] // 2
    order = left_ref.shape[2]
    for m, out in enumerate(outs):
        to = spot_ref[0] ^ m
        part = pl.ds(pl.multiple_of((to >> 1) * half, half), half)
        out[:half, :] = left_ref[to & 1, part, :]
        for t in range(0, order, half):
            out[half:, t : t + half] = right_ref[to & 1, t : t + half, part]


def unpack_kernel(spot_ref, *refs):
    got, out = refs[:-1], refs[-1]
    half = out.shape[0] // len(got)
    for m, ref in enumerate(got):
        out[m * half : (m + 1) * half, :] = ref[:half, :]


def update_kernel(spot_ref, own_ref, other_ref, left_ref, left2_ref, *refs):
    rights = refs[0:4]
    grad, update_ref, norm_ref, root, mixed = refs[4:]
    core, lane = spot_ref[1], spot_ref[2]
    owners, chips, piece, half = own_ref.shape
    order = grad.shape[0]
    for d in range(chips):
        mine = pl.multiple_of((2 * d + core) * half, half)
        theirs = pl.multiple_of((2 * d + 1 - core) * half, half)
        grad[:, pl.ds(mine, half)] = own_ref[:, d].reshape(order, half)
        grad[:, pl.ds(theirs, half)] = other_ref[:, d].reshape(order, half)
        to = pl.ds(pl.multiple_of((lane ^ d) * half, half), half)
        for t in range(0, order, half):
            root[t : t + half, to] = rights[d][half:, t : t + half]
    for t in range(0, order, 512):
        mixed[t : t + 512, :] = jnp.dot(grad[t : t + 512, :], root[...], preferred_element_type=F32).astype(BF16)
    total = jnp.zeros((8, 128), F32)
    count = half // piece
    for rows, which, first in ((left_ref, core, lane), (left2_ref, 1 - core, lane ^ 2)):
        part = jnp.dot(rows[...], mixed[...], preferred_element_type=F32).astype(BF16)
        wide = part.astype(F32)
        squares = jnp.sum((wide * wide).reshape(chips * half // 8, 8, chips * half), axis=0)
        for y in range(chips):
            total = total + squares[:, y * half : (y + 1) * half]
            for m in range(chips):
                block = part[m * half : (m + 1) * half, y * half : (y + 1) * half]
                spot = (first ^ m) * (2 * count) + which * count
                update_ref[pl.ds(spot, count), y] = block.reshape(count, piece, half)
    norm = jnp.sum(jnp.sum(total, axis=0, keepdims=True), axis=1, keepdims=True)
    norm_ref[...] = jnp.broadcast_to(norm, norm_ref.shape)


def product_kernel(spot_ref, grad, *refs):
    outs, (rows, columns) = refs[:-2], refs[-2:]
    core, lane = spot_ref[1], spot_ref[2]
    order = grad.shape[0]
    half = rows.shape[0] // 4
    for m in range(4):
        d = lane ^ m
        rows[m * half : (m + 1) * half, :] = grad[pl.ds(pl.multiple_of(d * 2 * half + core * half, half), half), :]
        columns[m * half : (m + 1) * half, :] = grad[:, pl.ds(pl.multiple_of((2 * d + core) * half, half), half)].T
    for n in range(0, order, 256):
        left = lax.dot_general(rows[...], grad[n : n + 256, :], (((1,), (1,)), ((), ())), preferred_element_type=F32)
        right = jnp.dot(columns[...], grad[:, n : n + 256], preferred_element_type=F32)
        for m, out in enumerate(outs):
            out[:half, n : n + 256] = left[m * half : (m + 1) * half].astype(BF16)
            out[half:, n : n + 256] = right[m * half : (m + 1) * half].astype(BF16)


def graft_kernel(spot_ref, update_ref, norm_ref, norm2_ref, after_ref, out_ref):
    scale = 1.0 / jnp.sqrt(norm_ref[0:1, :] + norm2_ref[0:1, :] + 1e-06)
    out_ref[...] = (update_ref[...].astype(F32) * scale[None, None]).astype(BF16)


def stat_kernel(spot_ref, p0, p1, p2, p3, left_ref, right_ref, new_left_ref, new_right_ref):
    half = left_ref.shape[1]
    for m, ref in enumerate((p0, p1, p2, p3)):

        @pl.when(pl.program_id(0) == m)
        def _():
            new_left_ref[0] = left_ref[0] + ref[:half, :].astype(F32)
            new_right_ref[0] = right_ref[0] + ref[half:, :].astype(F32)


def direction_kernel(slot_ref, values_ref, adam_ref, out_ref, wide, scales):
    row_blocks, rows, column_blocks, quarter = out_ref.shape
    half = quarter // 2
    size = wide.shape[0] // 2
    copies = jnp.sum(adam_ref[...].reshape(-1, 8, 128), axis=0)
    total = jnp.sqrt(copies[0:1, :])
    scales[...] = jnp.broadcast_to(total, scales.shape).T
    for b in range(row_blocks * column_blocks):
        at = spread_row(slot_ref[b])
        start = (b // column_blocks) * rows * column_blocks + b % column_blocks
        scale = scales[b : b + 1, :]
        wide[pl.ds(start, rows, stride=column_blocks), :] = values_ref[at].astype(F32) * scale
        wide[pl.ds(size + start, rows, stride=column_blocks), :] = values_ref[at + 4].astype(F32) * scale
    for h in range(2):
        part = wide[h * size : (h + 1) * size, :].reshape(row_blocks, rows, column_blocks, half)
        out_ref[..., h * half : (h + 1) * half] = part.astype(out_ref.dtype)


def body(gradient, second_moment, stat_left, stat_right, root_left, root_right, block_slot):
    owners = lax.axis_size("fsdp")
    chips = lax.axis_size("dp")
    devices = owners * chips
    row_blocks, piece_rows, column_blocks, quarter = gradient.shape
    blocks = row_blocks * column_blocks
    order = stat_left.shape[2]
    half = quarter // 2
    core = lax.axis_index("fsdp") % 2
    chip = lax.axis_index("dp")
    spot = jnp.stack([chip, core, 2 * core + chip % 2]).astype(jnp.int32)

    def matching(m, back):
        pairs = []
        for k in range(owners // 2):
            for c in range(2):
                for d in range(chips):
                    c2, j = (d ^ m) >> 1, (d ^ m) & 1
                    here = (2 * k + c) * chips + d
                    there = (2 * k + c2) * chips + 2 * c + j
                    pairs.append((there, here) if back else (here, there))
        return pairs

    swap = [(i, i ^ 1) for i in range(owners)]

    packed = local(
        pack_kernel, [shape((2 * half, order), BF16)] * chips, (spot, root_left, root_right),
        limit=5, moved=4 * MIB,
    )
    roots = [lax.ppermute(packed[m], AXES, matching(m, False)) for m in range(chips)]

    pieces = local(
        spread_kernel, shape((devices, piece_rows, half), BF16), (block_slot, gradient, packed[0]),
        scratch=[pltpu.VMEM((2 * blocks * piece_rows, half), F32)], limit=6, moved=MIB * 3 // 2,
    )
    own = lax.all_to_all(pieces, AXES, split_axis=0, concat_axis=0, tiled=True)

    new_second, sent = local(
        moment_kernel,
        [shape(second_moment.shape, F32), shape((8, 128), F32)],
        (block_slot, gradient, second_moment),
        scratch=[pltpu.VMEM((128, 128), F32)], limit=6, moved=MIB * 5 // 2,
    )
    adam = lax.all_gather(sent, AXES, axis=0, tiled=True)

    own, *roots = lax.optimization_barrier((own, *roots))
    left = local(unpack_kernel, shape((order // 2, order), BF16), (spot, *roots), limit=4, moved=2 * MIB)
    left2 = lax.ppermute(left, "fsdp", swap)
    other = lax.ppermute(own, "fsdp", swap)

    cut = (owners, chips, piece_rows, half)
    grad, update, norm = local(
        update_kernel,
        [shape((order, order), BF16), shape(cut, BF16), shape((8, 128), F32)],
        (spot, own.reshape(cut), other.reshape(cut), left, left2, *roots),
        scratch=[pltpu.VMEM((order, order // 2), BF16)] * 2,
        flops=2 * order * order * order, limit=18, moved=8 * MIB,
    )
    norm2 = lax.ppermute(norm, "fsdp", swap)
    products = local(
        product_kernel, [shape((2 * half, order), BF16)] * chips, (spot, grad),
        scratch=[pltpu.VMEM((order // 2, order), BF16)] * 2,
        flops=2 * order * order * order, limit=11, moved=4 * MIB,
    )
    update, adam = lax.optimization_barrier((update, adam))
    back = local(graft_kernel, shape(cut, BF16), (spot, update, norm, norm2, products[0]), limit=5, moved=2 * MIB)
    products = [lax.ppermute(products[m], AXES, matching(m, True)) for m in range(chips)]
    returned = lax.all_to_all(back.reshape(devices, piece_rows, half), AXES, split_axis=0, concat_axis=0, tiled=True)

    whole = pl.BlockSpec((2 * half, order), lambda m, s: (0, 0))
    piece = pl.BlockSpec((1, half, order), lambda m, s: ((s[0] ^ m) & 1, (s[0] ^ m) >> 1, 0))
    new_left, new_right = pl.pallas_call(
        stat_kernel,
        out_shape=[shape(stat_left.shape, F32), shape(stat_right.shape, F32)],
        grid_spec=pltpu.PrefetchScalarGridSpec(
            num_scalar_prefetch=1, grid=(chips,), in_specs=[whole] * chips + [piece] * 2, out_specs=[piece] * 2
        ),
        compiler_params=pltpu.CompilerParams(vmem_limit_bytes=10 * MIB),
        cost_estimate=pl.CostEstimate(flops=0, bytes_accessed=10 * MIB, transcendentals=0),
    )(spot, *products, stat_left, stat_right)

    direction = local(
        direction_kernel, shape(gradient.shape, gradient.dtype), (block_slot, returned, adam),
        scratch=[pltpu.VMEM((2 * blocks * piece_rows, half), F32), pltpu.VMEM((128, 128), F32)],
        limit=7, moved=2 * MIB,
    )
    return (new_left, new_right, new_second, direction)


def solution(mesh):
    placed = (
        P(None, "fsdp", None, "dp"),
        P(None, "fsdp", None, "dp"),
        P("fsdp", "dp", None),
        P("fsdp", "dp", None),
        P("fsdp", "dp", None),
        P("fsdp", None, "dp"),
        P(),
    )
    return jax.shard_map(
        body,
        mesh=mesh,
        in_specs=placed,
        out_specs=(
            P("fsdp", "dp", None),
            P("fsdp", "dp", None),
            P(None, "fsdp", None, "dp"),
            P(None, "fsdp", None, "dp"),
        ),
        check_vma=False,
    )
```

```python
import jax
import jax.numpy as jnp
from jax import lax
from jax.experimental import pallas as pl
from jax.experimental.pallas import tpu as pltpu
from jax.sharding import PartitionSpec as P

AXES = ("fsdp", "dp")
F32 = jnp.float32
BF16 = jnp.bfloat16
SMEM = pl.BlockSpec(memory_space=pltpu.SMEM)
VMEM = pl.BlockSpec(memory_space=pltpu.VMEM)
MIB = 1 << 20


def local(kernel, outs, inputs, scratch=(), limit=16, flops=0, moved=0):
    return pl.pallas_call(
        kernel,
        out_shape=outs,
        in_specs=[SMEM] + [VMEM] * (len(inputs) - 1),
        out_specs=jax.tree.map(lambda _: VMEM, outs),
        scratch_shapes=list(scratch),
        compiler_params=pltpu.CompilerParams(vmem_limit_bytes=limit * MIB),
        cost_estimate=pl.CostEstimate(flops=flops, bytes_accessed=moved, transcendentals=0),
    )(*inputs)


def shape(dims, dtype):
    return jax.ShapeDtypeStruct(dims, dtype)


def spread_row(slot):
    return ((slot >> 2) << 3) + (slot & 3)


def spread_kernel(slot_ref, grad_ref, out_ref, wide):
    row_blocks, rows, column_blocks, quarter = grad_ref.shape
    half = quarter // 2
    out_ref[...] = jnp.zeros_like(out_ref)
    size = wide.shape[0] // 2
    for h in range(2):
        wide[h * size : (h + 1) * size, :] = grad_ref[..., h * half : (h + 1) * half].astype(F32).reshape(size, half)
    for b in range(row_blocks * column_blocks):
        start = (b // column_blocks) * rows * column_blocks + b % column_blocks
        at = spread_row(slot_ref[b])
        out_ref[at] = wide[pl.ds(start, rows, stride=column_blocks), :].astype(BF16)
        out_ref[at + 4] = wide[pl.ds(size + start, rows, stride=column_blocks), :].astype(BF16)


def moment_kernel(slot_ref, grad_ref, second_ref, new_ref, sent_ref, part):
    row_blocks, _, column_blocks, _ = grad_ref.shape
    part[...] = jnp.zeros_like(part)
    for r in range(row_blocks):
        g = grad_ref[r].astype(F32)
        new = 0.9 * second_ref[r] + 0.1 * g * g
        new_ref[r] = new
        adam = g / (jnp.sqrt(new) + 1e-08)
        sums = jnp.sum(jnp.sum(adam * adam, axis=0), axis=1, keepdims=True)
        part[r * column_blocks : (r + 1) * column_blocks, :] = jnp.broadcast_to(sums, (column_blocks, 128))
    sent_ref[...] = part[...].T[0:8, :]


def pack_kernel(spot_ref, left_ref, right_ref, *outs):
    half = left_ref.shape[1] // 2
    order = left_ref.shape[2]
    for m, out in enumerate(outs):
        to = spot_ref[0] ^ m
        part = pl.ds(pl.multiple_of((to >> 1) * half, half), half)
        out[:half, :] = left_ref[to & 1, part, :]
        for t in range(0, order, half):
            out[half:, t : t + half] = right_ref[to & 1, t : t + half, part]


def unpack_kernel(spot_ref, *refs):
    got, out = refs[:-1], refs[-1]
    half = out.shape[0] // len(got)
    for m, ref in enumerate(got):
        out[m * half : (m + 1) * half, :] = ref[:half, :]


def update_kernel(spot_ref, slots_ref, own_ref, other_ref, left_ref, left2_ref, *refs):
    rights = refs[0:4]
    grad, update_ref, norm_ref, root, mixed = refs[4:]
    core, lane = spot_ref[1], spot_ref[2]
    owners, chips, piece, half = own_ref.shape
    order = grad.shape[0]
    for d in range(chips):
        mine = pl.multiple_of((2 * d + core) * half, half)
        theirs = pl.multiple_of((2 * d + 1 - core) * half, half)
        grad[:, pl.ds(mine, half)] = own_ref[:, d].reshape(order, half)
        grad[:, pl.ds(theirs, half)] = other_ref[:, d].reshape(order, half)
        to = pl.ds(pl.multiple_of((lane ^ d) * half, half), half)
        for t in range(0, order, half):
            root[t : t + half, to] = rights[d][half:, t : t + half]
    for t in range(0, order, 512):
        mixed[t : t + 512, :] = jnp.dot(grad[t : t + 512, :], root[...], preferred_element_type=F32).astype(BF16)
    total = jnp.zeros((8, 128), F32)
    count = half // piece
    for rows, which, first in ((left_ref, core, lane), (left2_ref, 1 - core, lane ^ 2)):
        part = jnp.dot(rows[...], mixed[...], preferred_element_type=F32).astype(BF16)
        wide = part.astype(F32)
        squares = jnp.sum((wide * wide).reshape(chips * half // 8, 8, chips * half), axis=0)
        for y in range(chips):
            total = total + squares[:, y * half : (y + 1) * half]
            for m in range(chips):
                block = part[m * half : (m + 1) * half, y * half : (y + 1) * half]
                spot = (first ^ m) * (2 * count) + which * count
                update_ref[pl.ds(spot, count), y] = block.reshape(count, piece, half)
    norm = jnp.sum(jnp.sum(total, axis=0, keepdims=True), axis=1, keepdims=True)
    norm_ref[...] = jnp.broadcast_to(jnp.where(slots_ref[...] == spot_ref[3], norm, 0.0), norm_ref.shape)


def product_kernel(spot_ref, grad, *refs):
    outs, (rows, columns) = refs[:-2], refs[-2:]
    core, lane = spot_ref[1], spot_ref[2]
    order = grad.shape[0]
    half = rows.shape[0] // 4
    for m in range(4):
        d = lane ^ m
        rows[m * half : (m + 1) * half, :] = grad[pl.ds(pl.multiple_of(d * 2 * half + core * half, half), half), :]
        columns[m * half : (m + 1) * half, :] = grad[:, pl.ds(pl.multiple_of((2 * d + core) * half, half), half)].T
    for n in range(0, order, 256):
        left = lax.dot_general(rows[...], grad[n : n + 256, :], (((1,), (1,)), ((), ())), preferred_element_type=F32)
        right = jnp.dot(columns[...], grad[:, n : n + 256], preferred_element_type=F32)
        for m, out in enumerate(outs):
            out[:half, n : n + 256] = left[m * half : (m + 1) * half].astype(BF16)
            out[half:, n : n + 256] = right[m * half : (m + 1) * half].astype(BF16)


def stat_kernel(spot_ref, p0, p1, p2, p3, left_ref, right_ref, new_left_ref, new_right_ref):
    half = left_ref.shape[1]
    for m, ref in enumerate((p0, p1, p2, p3)):

        @pl.when(pl.program_id(0) == m)
        def _():
            new_left_ref[0] = left_ref[0] + ref[:half, :].astype(F32)
            new_right_ref[0] = right_ref[0] + ref[half:, :].astype(F32)


def direction_kernel(slot_ref, values_ref, adam_ref, out_ref, wide, scales):
    row_blocks, rows, column_blocks, quarter = out_ref.shape
    half = quarter // 2
    size = wide.shape[0] // 2
    blocks = row_blocks * column_blocks
    total = jnp.sum(adam_ref[...].reshape(-1, 8, 128), axis=0)[0:1, :]
    scales[...] = jnp.broadcast_to(total, scales.shape).T
    scales[:blocks, :] = jnp.sqrt(scales[:blocks, :] / (scales[blocks : 2 * blocks, :] + 1e-06))
    for b in range(row_blocks * column_blocks):
        at = spread_row(slot_ref[b])
        start = (b // column_blocks) * rows * column_blocks + b % column_blocks
        scale = scales[b : b + 1, :]
        wide[pl.ds(start, rows, stride=column_blocks), :] = values_ref[at].astype(F32) * scale
        wide[pl.ds(size + start, rows, stride=column_blocks), :] = values_ref[at + 4].astype(F32) * scale
    for h in range(2):
        part = wide[h * size : (h + 1) * size, :].reshape(row_blocks, rows, column_blocks, half)
        out_ref[..., h * half : (h + 1) * half] = part.astype(out_ref.dtype)


def body(gradient, second_moment, stat_left, stat_right, root_left, root_right, block_slot):
    owners = lax.axis_size("fsdp")
    chips = lax.axis_size("dp")
    devices = owners * chips
    row_blocks, piece_rows, column_blocks, quarter = gradient.shape
    blocks = row_blocks * column_blocks
    order = stat_left.shape[2]
    half = quarter // 2
    core = lax.axis_index("fsdp") % 2
    chip = lax.axis_index("dp")
    slot = 4 * (lax.axis_index("fsdp") // 2) + chip
    spot = jnp.stack([chip, core, 2 * core + chip % 2, slot]).astype(jnp.int32)
    slots = jnp.concatenate([jnp.full((128 - blocks,), -1, jnp.int32), block_slot])[None]

    def matching(m, back):
        pairs = []
        for k in range(owners // 2):
            for c in range(2):
                for d in range(chips):
                    c2, j = (d ^ m) >> 1, (d ^ m) & 1
                    here = (2 * k + c) * chips + d
                    there = (2 * k + c2) * chips + 2 * c + j
                    pairs.append((there, here) if back else (here, there))
        return pairs

    swap = [(i, i ^ 1) for i in range(owners)]

    packed = local(
        pack_kernel, [shape((2 * half, order), BF16)] * chips, (spot, root_left, root_right),
        limit=5, moved=4 * MIB,
    )
    roots = [lax.ppermute(packed[m], AXES, matching(m, False)) for m in range(chips)]

    pieces = local(
        spread_kernel, shape((devices, piece_rows, half), BF16), (block_slot, gradient),
        scratch=[pltpu.VMEM((2 * blocks * piece_rows, half), F32)], limit=6, moved=MIB * 3 // 2,
    )
    own = lax.cond(
        block_slot[0] >= 0,
        lambda x: lax.all_to_all(x, AXES, split_axis=0, concat_axis=0, tiled=True),
        lambda x: x,
        pieces,
    )

    new_second, sent = local(
        moment_kernel,
        [shape(second_moment.shape, F32), shape((8, 128), F32)],
        (block_slot, gradient, second_moment),
        scratch=[pltpu.VMEM((128, 128), F32)], limit=6, moved=MIB * 5 // 2,
    )
    own, *roots = lax.optimization_barrier((own, *roots))
    left = local(unpack_kernel, shape((order // 2, order), BF16), (spot, *roots), limit=4, moved=2 * MIB)
    left2 = lax.ppermute(left, "fsdp", swap)
    other = lax.ppermute(own, "fsdp", swap)

    cut = (owners, chips, piece_rows, half)
    grad, update, norm = local(
        update_kernel,
        [shape((order, order), BF16), shape(cut, BF16), shape((8, 128), F32)],
        (spot, slots, own.reshape(cut), other.reshape(cut), left, left2, *roots),
        scratch=[pltpu.VMEM((order, order // 2), BF16)] * 2,
        flops=2 * order * order * order, limit=18, moved=8 * MIB,
    )
    products = local(
        product_kernel, [shape((2 * half, order), BF16)] * chips, (spot, grad),
        scratch=[pltpu.VMEM((order // 2, order), BF16)] * 2,
        flops=2 * order * order * order, limit=11, moved=4 * MIB,
    )
    update, *products = lax.optimization_barrier((update, *products))
    products = [lax.ppermute(products[m], AXES, matching(m, True)) for m in range(chips)]
    returned = lax.all_to_all(update.reshape(devices, piece_rows, half), AXES, split_axis=0, concat_axis=0, tiled=True)

    near = owners // 8
    groups = [
        [[near_at * 8 + i for i in range(8)] for near_at in range(near)],
        [[i + 8 * z for z in range(near)] for i in range(8)],
    ]
    adam = lax.all_gather(sent + norm, "dp", axis=0, tiled=False).sum(axis=0)
    adam = lax.all_gather(adam, "fsdp", axis_index_groups=groups[0], axis=0, tiled=False).sum(axis=0)
    adam = lax.all_gather(adam, "fsdp", axis_index_groups=groups[1], axis=0, tiled=True)


    whole = pl.BlockSpec((2 * half, order), lambda m, s: (0, 0))
    piece = pl.BlockSpec((1, half, order), lambda m, s: ((s[0] ^ m) & 1, (s[0] ^ m) >> 1, 0))
    new_left, new_right = pl.pallas_call(
        stat_kernel,
        out_shape=[shape(stat_left.shape, F32), shape(stat_right.shape, F32)],
        grid_spec=pltpu.PrefetchScalarGridSpec(
            num_scalar_prefetch=1, grid=(chips,), in_specs=[whole] * chips + [piece] * 2, out_specs=[piece] * 2
        ),
        compiler_params=pltpu.CompilerParams(vmem_limit_bytes=10 * MIB),
        cost_estimate=pl.CostEstimate(flops=0, bytes_accessed=10 * MIB, transcendentals=0),
    )(spot, *products, stat_left, stat_right)

    direction = local(
        direction_kernel, shape(gradient.shape, gradient.dtype), (block_slot, returned, adam),
        scratch=[pltpu.VMEM((2 * blocks * piece_rows, half), F32), pltpu.VMEM((128, 128), F32)],
        limit=7, moved=2 * MIB,
    )
    return (new_left, new_right, new_second, direction)


def solution(mesh):
    placed = (
        P(None, "fsdp", None, "dp"),
        P(None, "fsdp", None, "dp"),
        P("fsdp", "dp", None),
        P("fsdp", "dp", None),
        P("fsdp", "dp", None),
        P("fsdp", None, "dp"),
        P(),
    )
    return jax.shard_map(
        body,
        mesh=mesh,
        in_specs=placed,
        out_specs=(
            P("fsdp", "dp", None),
            P("fsdp", "dp", None),
            P(None, "fsdp", None, "dp"),
            P(None, "fsdp", None, "dp"),
        ),
        check_vma=False,
    )
```

```python
import jax
import jax.numpy as jnp
from jax import lax
from jax.experimental import pallas as pl
from jax.experimental.pallas import tpu as pltpu
from jax.sharding import PartitionSpec as P

AXES = ("fsdp", "dp")
F32 = jnp.float32
BF16 = jnp.bfloat16
SMEM = pl.BlockSpec(memory_space=pltpu.SMEM)
VMEM = pl.BlockSpec(memory_space=pltpu.VMEM)
MIB = 1 << 20


def local(kernel, outs, inputs, scratch=(), limit=16, flops=0, moved=0):
    return pl.pallas_call(
        kernel,
        out_shape=outs,
        in_specs=[SMEM] + [VMEM] * (len(inputs) - 1),
        out_specs=jax.tree.map(lambda _: VMEM, outs),
        scratch_shapes=list(scratch),
        compiler_params=pltpu.CompilerParams(vmem_limit_bytes=limit * MIB),
        cost_estimate=pl.CostEstimate(flops=flops, bytes_accessed=moved, transcendentals=0),
    )(*inputs)


def shape(dims, dtype):
    return jax.ShapeDtypeStruct(dims, dtype)


def spread_row(slot):
    return ((slot >> 2) << 3) + (slot & 3)


def spread_kernel(slot_ref, grad_ref, out_ref, wide):
    row_blocks, rows, column_blocks, quarter = grad_ref.shape
    half = quarter // 2
    out_ref[...] = jnp.zeros_like(out_ref)
    size = wide.shape[0] // 2
    for h in range(2):
        wide[h * size : (h + 1) * size, :] = grad_ref[..., h * half : (h + 1) * half].astype(F32).reshape(size, half)
    for b in range(row_blocks * column_blocks):
        start = (b // column_blocks) * rows * column_blocks + b % column_blocks
        at = spread_row(slot_ref[b])
        out_ref[at] = wide[pl.ds(start, rows, stride=column_blocks), :].astype(BF16)
        out_ref[at + 4] = wide[pl.ds(size + start, rows, stride=column_blocks), :].astype(BF16)


def moment_kernel(slot_ref, grad_ref, second_ref, new_ref, sent_ref, part):
    row_blocks, _, column_blocks, _ = grad_ref.shape
    sent_ref[...] = jnp.zeros_like(sent_ref)
    for r in range(row_blocks):
        g = grad_ref[r].astype(F32)
        new = 0.9 * second_ref[r] + 0.1 * g * g
        new_ref[r] = new
        adam = g / (jnp.sqrt(new) + 1e-08)
        sums = jnp.sum(jnp.sum(adam * adam, axis=0), axis=1, keepdims=True)
        part[r * column_blocks : (r + 1) * column_blocks, :] = jnp.broadcast_to(sums, (column_blocks, 128))
    for b in range(row_blocks * column_blocks):
        at = spread_row(slot_ref[b])
        sent_ref[at] = part[b : b + 1, :]
        sent_ref[at + 4] = part[b : b + 1, :]


def pack_kernel(spot_ref, left_ref, right_ref, *outs):
    half = left_ref.shape[1] // 2
    order = left_ref.shape[2]
    for m, out in enumerate(outs):
        to = spot_ref[0] ^ m
        part = pl.ds(pl.multiple_of((to >> 1) * half, half), half)
        out[:half, :] = left_ref[to & 1, part, :]
        for t in range(0, order, half):
            out[half:, t : t + half] = right_ref[to & 1, t : t + half, part]


def unpack_kernel(spot_ref, *refs):
    got, (left_ref, right_ref) = refs[:-2], refs[-2:]
    half = right_ref.shape[1]
    for m, ref in enumerate(got):
        left_ref[m * half : (m + 1) * half, :] = ref[:half, :]
        right_ref[m] = ref[half:, :]


def update_kernel(spot_ref, own_ref, other_ref, left_ref, left2_ref, right_ref, *refs):
    grad, update_ref, norm_ref, root, mixed = refs
    core, lane = spot_ref[1], spot_ref[2]
    owners, chips, piece, half = own_ref.shape
    order = grad.shape[0]
    for d in range(chips):
        mine = pl.multiple_of((2 * d + core) * half, half)
        theirs = pl.multiple_of((2 * d + 1 - core) * half, half)
        grad[:, pl.ds(mine, half)] = own_ref[:, d].reshape(order, half)
        grad[:, pl.ds(theirs, half)] = other_ref[:, d].reshape(order, half)
        to = pl.ds(pl.multiple_of((lane ^ d) * half, half), half)
        for t in range(0, order, half):
            root[t : t + half, to] = right_ref[d, :, t : t + half]
    for t in range(0, order, 512):
        mixed[t : t + 512, :] = jnp.dot(grad[t : t + 512, :], root[...], preferred_element_type=F32).astype(BF16)
    total = jnp.zeros((8, 128), F32)
    count = half // piece
    for rows, which, first in ((left_ref, core, lane), (left2_ref, 1 - core, lane ^ 2)):
        part = jnp.dot(rows[...], mixed[...], preferred_element_type=F32).astype(BF16)
        wide = part.astype(F32)
        squares = jnp.sum((wide * wide).reshape(chips * half // 8, 8, chips * half), axis=0)
        for y in range(chips):
            total = total + squares[:, y * half : (y + 1) * half]
            for m in range(chips):
                block = part[m * half : (m + 1) * half, y * half : (y + 1) * half]
                spot = (first ^ m) * (2 * count) + which * count
                update_ref[pl.ds(spot, count), y] = block.reshape(count, piece, half)
    norm = jnp.sum(jnp.sum(total, axis=0, keepdims=True), axis=1, keepdims=True)
    norm_ref[...] = jnp.broadcast_to(norm, norm_ref.shape)


def product_kernel(spot_ref, grad, *refs):
    outs, (rows, columns) = refs[:-2], refs[-2:]
    core, lane = spot_ref[1], spot_ref[2]
    order = grad.shape[0]
    half = rows.shape[0] // 4
    for m in range(4):
        d = lane ^ m
        rows[m * half : (m + 1) * half, :] = grad[pl.ds(pl.multiple_of(d * 2 * half + core * half, half), half), :]
        columns[m * half : (m + 1) * half, :] = grad[:, pl.ds(pl.multiple_of((2 * d + core) * half, half), half)].T
    for n in range(0, order, 256):
        left = lax.dot_general(rows[...], grad[n : n + 256, :], (((1,), (1,)), ((), ())), preferred_element_type=F32)
        right = jnp.dot(columns[...], grad[:, n : n + 256], preferred_element_type=F32)
        for m, out in enumerate(outs):
            out[:half, n : n + 256] = left[m * half : (m + 1) * half].astype(BF16)
            out[half:, n : n + 256] = right[m * half : (m + 1) * half].astype(BF16)


def graft_kernel(spot_ref, update_ref, norm_ref, norm2_ref, adam_ref, out_ref):
    adam = jnp.sum(adam_ref[...], axis=0)
    scale = jnp.sqrt(adam / (norm_ref[0:1, :] + norm2_ref[0:1, :] + 1e-06))
    out_ref[...] = (update_ref[...].astype(F32) * scale[None, None]).astype(BF16)


def stat_kernel(spot_ref, p0, p1, p2, p3, left_ref, right_ref, new_left_ref, new_right_ref):
    half = left_ref.shape[1]
    for m, ref in enumerate((p0, p1, p2, p3)):

        @pl.when(pl.program_id(0) == m)
        def _():
            new_left_ref[0] = left_ref[0] + ref[:half, :].astype(F32)
            new_right_ref[0] = right_ref[0] + ref[half:, :].astype(F32)


def direction_kernel(slot_ref, values_ref, out_ref, wide):
    row_blocks, rows, column_blocks, quarter = out_ref.shape
    half = quarter // 2
    size = wide.shape[0] // 2
    for b in range(row_blocks * column_blocks):
        at = spread_row(slot_ref[b])
        start = (b // column_blocks) * rows * column_blocks + b % column_blocks
        wide[pl.ds(start, rows, stride=column_blocks), :] = values_ref[at].astype(F32)
        wide[pl.ds(size + start, rows, stride=column_blocks), :] = values_ref[at + 4].astype(F32)
    for h in range(2):
        part = wide[h * size : (h + 1) * size, :].reshape(row_blocks, rows, column_blocks, half)
        out_ref[..., h * half : (h + 1) * half] = part.astype(out_ref.dtype)


def body(gradient, second_moment, stat_left, stat_right, root_left, root_right, block_slot):
    owners = lax.axis_size("fsdp")
    chips = lax.axis_size("dp")
    devices = owners * chips
    row_blocks, piece_rows, column_blocks, quarter = gradient.shape
    blocks = row_blocks * column_blocks
    order = stat_left.shape[2]
    half = quarter // 2
    core = lax.axis_index("fsdp") % 2
    chip = lax.axis_index("dp")
    spot = jnp.stack([chip, core, 2 * core + chip % 2]).astype(jnp.int32)

    def matching(m, back):
        pairs = []
        for k in range(owners // 2):
            for c in range(2):
                for d in range(chips):
                    c2, j = (d ^ m) >> 1, (d ^ m) & 1
                    here = (2 * k + c) * chips + d
                    there = (2 * k + c2) * chips + 2 * c + j
                    pairs.append((there, here) if back else (here, there))
        return pairs

    swap = [(i, i ^ 1) for i in range(owners)]

    packed = local(
        pack_kernel, [shape((2 * half, order), BF16)] * chips, (spot, root_left, root_right),
        limit=5, moved=4 * MIB,
    )
    roots = [lax.ppermute(packed[m], AXES, matching(m, False)) for m in range(chips)]

    new_second, sent = local(
        moment_kernel,
        [shape(second_moment.shape, F32), shape((devices, 1, 128), F32)],
        (block_slot, gradient, second_moment),
        scratch=[pltpu.VMEM((blocks, 128), F32)], limit=6, moved=MIB * 5 // 2,
    )
    adam = lax.all_to_all(sent, AXES, split_axis=0, concat_axis=0, tiled=True)

    pieces = local(
        spread_kernel, shape((devices, piece_rows, half), BF16), (block_slot, gradient),
        scratch=[pltpu.VMEM((2 * blocks * piece_rows, half), F32)], limit=6, moved=MIB * 3 // 2,
    )
    own = lax.cond(
        block_slot[0] >= 0,
        lambda x: lax.all_to_all(x, AXES, split_axis=0, concat_axis=0, tiled=True),
        lambda x: x,
        pieces,
    )

    own, *roots = lax.optimization_barrier((own, *roots))
    left, right = local(
        unpack_kernel, [shape((order // 2, order), BF16), shape((chips, half, order), BF16)], (spot, *roots),
        limit=5, moved=4 * MIB,
    )
    left2 = lax.ppermute(left, "fsdp", swap)
    other = lax.ppermute(own, "fsdp", swap)

    cut = (owners, chips, piece_rows, half)
    grad, update, norm = local(
        update_kernel,
        [shape((order, order), BF16), shape(cut, BF16), shape((8, 128), F32)],
        (spot, own.reshape(cut), other.reshape(cut), left, left2, right),
        scratch=[pltpu.VMEM((order, order // 2), BF16)] * 2,
        flops=2 * order * order * order, limit=18, moved=8 * MIB,
    )
    norm2 = lax.ppermute(norm, "fsdp", swap)
    products = local(
        product_kernel, [shape((2 * half, order), BF16)] * chips, (spot, grad),
        scratch=[pltpu.VMEM((order // 2, order), BF16)] * 2,
        flops=2 * order * order * order, limit=11, moved=4 * MIB,
    )
    update, *products = lax.optimization_barrier((update, *products))
    back = local(graft_kernel, shape(cut, BF16), (spot, update, norm, norm2, adam), limit=5, moved=2 * MIB)
    products = [lax.ppermute(products[m], AXES, matching(m, True)) for m in range(chips)]
    returned = lax.all_to_all(back.reshape(devices, piece_rows, half), AXES, split_axis=0, concat_axis=0, tiled=True)

    whole = pl.BlockSpec((2 * half, order), lambda m, s: (0, 0))
    piece = pl.BlockSpec((1, half, order), lambda m, s: ((s[0] ^ m) & 1, (s[0] ^ m) >> 1, 0))
    new_left, new_right = pl.pallas_call(
        stat_kernel,
        out_shape=[shape(stat_left.shape, F32), shape(stat_right.shape, F32)],
        grid_spec=pltpu.PrefetchScalarGridSpec(
            num_scalar_prefetch=1, grid=(chips,), in_specs=[whole] * chips + [piece] * 2, out_specs=[piece] * 2
        ),
        compiler_params=pltpu.CompilerParams(vmem_limit_bytes=10 * MIB),
        cost_estimate=pl.CostEstimate(flops=0, bytes_accessed=10 * MIB, transcendentals=0),
    )(spot, *products, stat_left, stat_right)

    direction = local(
        direction_kernel, shape(gradient.shape, gradient.dtype), (block_slot, returned),
        scratch=[pltpu.VMEM((2 * blocks * piece_rows, half), F32)],
        limit=7, moved=2 * MIB,
    )
    return (new_left, new_right, new_second, direction)


def solution(mesh):
    placed = (
        P(None, "fsdp", None, "dp"),
        P(None, "fsdp", None, "dp"),
        P("fsdp", "dp", None),
        P("fsdp", "dp", None),
        P("fsdp", "dp", None),
        P("fsdp", None, "dp"),
        P(),
    )
    return jax.shard_map(
        body,
        mesh=mesh,
        in_specs=placed,
        out_specs=(
            P("fsdp", "dp", None),
            P("fsdp", "dp", None),
            P(None, "fsdp", None, "dp"),
            P(None, "fsdp", None, "dp"),
        ),
        check_vma=False,
    )
```

```python
import jax
import jax.numpy as jnp
from jax import lax
from jax.experimental import pallas as pl
from jax.experimental.pallas import tpu as pltpu
from jax.sharding import PartitionSpec as P

AXES = ("fsdp", "dp")
F32 = jnp.float32
BF16 = jnp.bfloat16
SMEM = pl.BlockSpec(memory_space=pltpu.SMEM)
VMEM = pl.BlockSpec(memory_space=pltpu.VMEM)
MIB = 1 << 20


def local(kernel, outs, inputs, scratch=(), limit=16, flops=0, moved=0):
    return pl.pallas_call(
        kernel,
        out_shape=outs,
        in_specs=[SMEM] + [VMEM] * (len(inputs) - 1),
        out_specs=jax.tree.map(lambda _: VMEM, outs),
        scratch_shapes=list(scratch),
        compiler_params=pltpu.CompilerParams(vmem_limit_bytes=limit * MIB),
        cost_estimate=pl.CostEstimate(flops=flops, bytes_accessed=moved, transcendentals=0),
    )(*inputs)


def shape(dims, dtype):
    return jax.ShapeDtypeStruct(dims, dtype)


def spread_row(slot):
    return ((slot >> 2) << 3) + (slot & 3)


def spread_kernel(slot_ref, grad_ref, out_ref, wide):
    row_blocks, rows, column_blocks, quarter = grad_ref.shape
    half = quarter // 2
    out_ref[...] = jnp.zeros_like(out_ref)
    size = wide.shape[0] // 2
    for h in range(2):
        wide[h * size : (h + 1) * size, :] = grad_ref[..., h * half : (h + 1) * half].astype(F32).reshape(size, half)
    for b in range(row_blocks * column_blocks):
        start = (b // column_blocks) * rows * column_blocks + b % column_blocks
        at = spread_row(slot_ref[b])
        out_ref[at] = wide[pl.ds(start, rows, stride=column_blocks), :].astype(BF16)
        out_ref[at + 4] = wide[pl.ds(size + start, rows, stride=column_blocks), :].astype(BF16)


def moment_kernel(slot_ref, grad_ref, second_ref, after_ref, new_ref, sent_ref, part):
    row_blocks, _, column_blocks, _ = grad_ref.shape
    part[...] = jnp.zeros_like(part)
    for r in range(row_blocks):
        g = grad_ref[r].astype(F32)
        new = 0.9 * second_ref[r] + 0.1 * g * g
        new_ref[r] = new
        adam = g / (jnp.sqrt(new) + 1e-08)
        sums = jnp.sum(jnp.sum(adam * adam, axis=0), axis=1, keepdims=True)
        part[r * column_blocks : (r + 1) * column_blocks, :] = jnp.broadcast_to(sums, (column_blocks, 128))
    sent_ref[...] = part[...].T[0:8, :]


def pack_kernel(spot_ref, left_ref, right_ref, *outs):
    half = left_ref.shape[1] // 2
    order = left_ref.shape[2]
    for m, out in enumerate(outs):
        to = spot_ref[0] ^ m
        part = pl.ds(pl.multiple_of((to >> 1) * half, half), half)
        out[:half, :] = left_ref[to & 1, part, :]
        for t in range(0, order, half):
            out[half:, t : t + half] = right_ref[to & 1, t : t + half, part]


def unpack_kernel(spot_ref, *refs):
    got, out = refs[:-1], refs[-1]
    half = out.shape[0] // len(got)
    for m, ref in enumerate(got):
        out[m * half : (m + 1) * half, :] = ref[:half, :]


def update_kernel(spot_ref, own_ref, other_ref, left_ref, left2_ref, *refs):
    rights = refs[0:4]
    grad, update_ref, norm_ref, root, mixed = refs[4:]
    core, lane = spot_ref[1], spot_ref[2]
    owners, chips, piece, half = own_ref.shape
    order = grad.shape[0]
    for d in range(chips):
        mine = pl.multiple_of((2 * d + core) * half, half)
        theirs = pl.multiple_of((2 * d + 1 - core) * half, half)
        grad[:, pl.ds(mine, half)] = own_ref[:, d].reshape(order, half)
        grad[:, pl.ds(theirs, half)] = other_ref[:, d].reshape(order, half)
        to = pl.ds(pl.multiple_of((lane ^ d) * half, half), half)
        for t in range(0, order, half):
            root[t : t + half, to] = rights[d][half:, t : t + half]
    for t in range(0, order, 512):
        mixed[t : t + 512, :] = jnp.dot(grad[t : t + 512, :], root[...], preferred_element_type=F32).astype(BF16)
    total = jnp.zeros((8, 128), F32)
    count = half // piece
    for rows, which, first in ((left_ref, core, lane), (left2_ref, 1 - core, lane ^ 2)):
        part = jnp.dot(rows[...], mixed[...], preferred_element_type=F32).astype(BF16)
        wide = part.astype(F32)
        squares = jnp.sum((wide * wide).reshape(chips * half // 8, 8, chips * half), axis=0)
        for y in range(chips):
            total = total + squares[:, y * half : (y + 1) * half]
            for m in range(chips):
                block = part[m * half : (m + 1) * half, y * half : (y + 1) * half]
                spot = (first ^ m) * (2 * count) + which * count
                update_ref[pl.ds(spot, count), y] = block.reshape(count, piece, half)
    norm = jnp.sum(jnp.sum(total, axis=0, keepdims=True), axis=1, keepdims=True)
    norm_ref[...] = jnp.broadcast_to(norm, norm_ref.shape)


def product_kernel(spot_ref, grad, *refs):
    outs, (rows, columns) = refs[:-2], refs[-2:]
    core, lane = spot_ref[1], spot_ref[2]
    order = grad.shape[0]
    half = rows.shape[0] // 4
    for m in range(4):
        d = lane ^ m
        rows[m * half : (m + 1) * half, :] = grad[pl.ds(pl.multiple_of(d * 2 * half + core * half, half), half), :]
        columns[m * half : (m + 1) * half, :] = grad[:, pl.ds(pl.multiple_of((2 * d + core) * half, half), half)].T
    for n in range(0, order, 256):
        left = lax.dot_general(rows[...], grad[n : n + 256, :], (((1,), (1,)), ((), ())), preferred_element_type=F32)
        right = jnp.dot(columns[...], grad[:, n : n + 256], preferred_element_type=F32)
        for m, out in enumerate(outs):
            out[:half, n : n + 256] = left[m * half : (m + 1) * half].astype(BF16)
            out[half:, n : n + 256] = right[m * half : (m + 1) * half].astype(BF16)


def graft_kernel(spot_ref, update_ref, norm_ref, norm2_ref, out_ref):
    scale = 1.0 / jnp.sqrt(norm_ref[0:1, :] + norm2_ref[0:1, :] + 1e-06)
    out_ref[...] = (update_ref[...].astype(F32) * scale[None, None]).astype(BF16)


def stat_kernel(spot_ref, p0, p1, p2, p3, left_ref, right_ref, new_left_ref, new_right_ref):
    half = left_ref.shape[1]
    for m, ref in enumerate((p0, p1, p2, p3)):

        @pl.when(pl.program_id(0) == m)
        def _():
            new_left_ref[0] = left_ref[0] + ref[:half, :].astype(F32)
            new_right_ref[0] = right_ref[0] + ref[half:, :].astype(F32)


def direction_kernel(slot_ref, values_ref, adam_ref, out_ref, wide, scales):
    row_blocks, rows, column_blocks, quarter = out_ref.shape
    half = quarter // 2
    size = wide.shape[0] // 2
    copies = jnp.sum(adam_ref[...].reshape(-1, 8, 128), axis=0)
    total = jnp.sqrt(jnp.sum(copies, axis=0, keepdims=True) * (1.0 / 8))
    scales[...] = jnp.broadcast_to(total, scales.shape).T
    for b in range(row_blocks * column_blocks):
        at = spread_row(slot_ref[b])
        start = (b // column_blocks) * rows * column_blocks + b % column_blocks
        scale = scales[b : b + 1, :]
        wide[pl.ds(start, rows, stride=column_blocks), :] = values_ref[at].astype(F32) * scale
        wide[pl.ds(size + start, rows, stride=column_blocks), :] = values_ref[at + 4].astype(F32) * scale
    for h in range(2):
        part = wide[h * size : (h + 1) * size, :].reshape(row_blocks, rows, column_blocks, half)
        out_ref[..., h * half : (h + 1) * half] = part.astype(out_ref.dtype)


def body(gradient, second_moment, stat_left, stat_right, root_left, root_right, block_slot):
    owners = lax.axis_size("fsdp")
    chips = lax.axis_size("dp")
    devices = owners * chips
    row_blocks, piece_rows, column_blocks, quarter = gradient.shape
    blocks = row_blocks * column_blocks
    order = stat_left.shape[2]
    half = quarter // 2
    core = lax.axis_index("fsdp") % 2
    chip = lax.axis_index("dp")
    spot = jnp.stack([chip, core, 2 * core + chip % 2]).astype(jnp.int32)

    def matching(m, back):
        pairs = []
        for k in range(owners // 2):
            for c in range(2):
                for d in range(chips):
                    c2, j = (d ^ m) >> 1, (d ^ m) & 1
                    here = (2 * k + c) * chips + d
                    there = (2 * k + c2) * chips + 2 * c + j
                    pairs.append((there, here) if back else (here, there))
        return pairs

    swap = [(i, i ^ 1) for i in range(owners)]

    packed = local(
        pack_kernel, [shape((2 * half, order), BF16)] * chips, (spot, root_left, root_right),
        limit=5, moved=4 * MIB,
    )
    roots = [lax.ppermute(packed[m], AXES, matching(m, False)) for m in range(chips)]

    new_second, sent = local(
        moment_kernel,
        [shape(second_moment.shape, F32), shape((8, 128), F32)],
        (block_slot, gradient, second_moment, packed[0]),
        scratch=[pltpu.VMEM((128, 128), F32)], limit=6, moved=MIB * 5 // 2,
    )
    adam = lax.all_gather(sent, AXES, axis=0, tiled=True)

    pieces = local(
        spread_kernel, shape((devices, piece_rows, half), BF16), (block_slot, gradient),
        scratch=[pltpu.VMEM((2 * blocks * piece_rows, half), F32)], limit=6, moved=MIB * 3 // 2,
    )
    own = lax.cond(
        block_slot[0] >= 0,
        lambda x: lax.all_to_all(x, AXES, split_axis=0, concat_axis=0, tiled=True),
        lambda x: x,
        pieces,
    )

    own, *roots = lax.optimization_barrier((own, *roots))
    left = local(unpack_kernel, shape((order // 2, order), BF16), (spot, *roots), limit=4, moved=2 * MIB)
    left2 = lax.ppermute(left, "fsdp", swap)
    other = lax.ppermute(own, "fsdp", swap)

    cut = (owners, chips, piece_rows, half)
    grad, update, norm = local(
        update_kernel,
        [shape((order, order), BF16), shape(cut, BF16), shape((8, 128), F32)],
        (spot, own.reshape(cut), other.reshape(cut), left, left2, *roots),
        scratch=[pltpu.VMEM((order, order // 2), BF16)] * 2,
        flops=2 * order * order * order, limit=18, moved=8 * MIB,
    )
    norm2 = lax.ppermute(norm, "fsdp", swap)
    products = local(
        product_kernel, [shape((2 * half, order), BF16)] * chips, (spot, grad),
        scratch=[pltpu.VMEM((order // 2, order), BF16)] * 2,
        flops=2 * order * order * order, limit=11, moved=4 * MIB,
    )
    update, *products = lax.optimization_barrier((update, *products))
    back = local(graft_kernel, shape(cut, BF16), (spot, update, norm, norm2), limit=5, moved=2 * MIB)

    def home(x, parts):
        parts = [lax.ppermute(part, AXES, matching(m, True)) for m, part in enumerate(parts)]
        return lax.all_to_all(x, AXES, split_axis=0, concat_axis=0, tiled=True), parts

    returned, products = lax.cond(
        block_slot[0] >= 0, home, lambda x, parts: (x, parts), back.reshape(devices, piece_rows, half), products
    )

    whole = pl.BlockSpec((2 * half, order), lambda m, s: (0, 0))
    piece = pl.BlockSpec((1, half, order), lambda m, s: ((s[0] ^ m) & 1, (s[0] ^ m) >> 1, 0))
    new_left, new_right = pl.pallas_call(
        stat_kernel,
        out_shape=[shape(stat_left.shape, F32), shape(stat_right.shape, F32)],
        grid_spec=pltpu.PrefetchScalarGridSpec(
            num_scalar_prefetch=1, grid=(chips,), in_specs=[whole] * chips + [piece] * 2, out_specs=[piece] * 2
        ),
        compiler_params=pltpu.CompilerParams(vmem_limit_bytes=10 * MIB),
        cost_estimate=pl.CostEstimate(flops=0, bytes_accessed=10 * MIB, transcendentals=0),
    )(spot, *products, stat_left, stat_right)

    direction = local(
        direction_kernel, shape(gradient.shape, gradient.dtype), (block_slot, returned, adam),
        scratch=[pltpu.VMEM((2 * blocks * piece_rows, half), F32), pltpu.VMEM((128, 128), F32)],
        limit=7, moved=2 * MIB,
    )
    return (new_left, new_right, new_second, direction)


def solution(mesh):
    placed = (
        P(None, "fsdp", None, "dp"),
        P(None, "fsdp", None, "dp"),
        P("fsdp", "dp", None),
        P("fsdp", "dp", None),
        P("fsdp", "dp", None),
        P("fsdp", None, "dp"),
        P(),
    )
    return jax.shard_map(
        body,
        mesh=mesh,
        in_specs=placed,
        out_specs=(
            P("fsdp", "dp", None),
            P("fsdp", "dp", None),
            P(None, "fsdp", None, "dp"),
            P(None, "fsdp", None, "dp"),
        ),
        check_vma=False,
    )
```

```python
import functools

import jax
import jax.numpy as jnp
from jax import lax
from jax.experimental import pallas as pl
from jax.experimental.pallas import tpu as pltpu
from jax.sharding import PartitionSpec as P

AXES = ("fsdp", "dp")
F32 = jnp.float32
BF16 = jnp.bfloat16
SMEM = pl.BlockSpec(memory_space=pltpu.SMEM)
VMEM = pl.BlockSpec(memory_space=pltpu.VMEM)
MIB = 1 << 20


def local(kernel, outs, inputs, scratch=(), limit=16, flops=0, moved=0):
    return pl.pallas_call(
        kernel,
        out_shape=outs,
        in_specs=[SMEM] + [VMEM] * (len(inputs) - 1),
        out_specs=jax.tree.map(lambda _: VMEM, outs),
        scratch_shapes=list(scratch),
        compiler_params=pltpu.CompilerParams(vmem_limit_bytes=limit * MIB),
        cost_estimate=pl.CostEstimate(flops=flops, bytes_accessed=moved, transcendentals=0),
    )(*inputs)


def shape(dims, dtype):
    return jax.ShapeDtypeStruct(dims, dtype)


def spread_row(slot):
    return ((slot >> 2) << 3) + (slot & 3)


def spread_kernel(slot_ref, grad_ref, out_ref, wide):
    row_blocks, rows, column_blocks, quarter = grad_ref.shape
    half = quarter // 2
    out_ref[...] = jnp.zeros_like(out_ref)
    size = wide.shape[0] // 2
    for h in range(2):
        wide[h * size : (h + 1) * size, :] = grad_ref[..., h * half : (h + 1) * half].astype(F32).reshape(size, half)
    for b in range(row_blocks * column_blocks):
        start = (b // column_blocks) * rows * column_blocks + b % column_blocks
        at = spread_row(slot_ref[b])
        out_ref[at] = wide[pl.ds(start, rows, stride=column_blocks), :].astype(BF16)
        out_ref[at + 4] = wide[pl.ds(size + start, rows, stride=column_blocks), :].astype(BF16)


def moment_kernel(slot_ref, grad_ref, second_ref, new_ref, sent_ref, part):
    row_blocks, _, column_blocks, _ = grad_ref.shape
    sent_ref[...] = jnp.zeros_like(sent_ref)
    for r in range(row_blocks):
        g = grad_ref[r].astype(F32)
        new = 0.9 * second_ref[r] + 0.1 * g * g
        new_ref[r] = new
        adam = g / (jnp.sqrt(new) + 1e-08)
        sums = jnp.sum(jnp.sum(adam * adam, axis=0), axis=1, keepdims=True)
        part[r * column_blocks : (r + 1) * column_blocks, :] = jnp.broadcast_to(sums, (column_blocks, 128))
    for b in range(row_blocks * column_blocks):
        at = spread_row(slot_ref[b])
        sent_ref[at] = part[b : b + 1, :]
        sent_ref[at + 4] = part[b : b + 1, :]


def pack_kernel(spot_ref, left_ref, right_ref, *refs):
    outs, sems = refs[:-1], refs[-1]
    half = left_ref.shape[1] // 2
    order = left_ref.shape[2]
    copies = []
    for m, out in enumerate(outs):
        to = spot_ref[0] ^ m
        part = pl.ds(pl.multiple_of((to >> 1) * half, half), half)
        copies.append((left_ref.at[to & 1, part], out.at[pl.ds(0, half)]))
        for t in range(0, order, half):
            copies.append((right_ref.at[to & 1, pl.ds(t, half), part], out.at[pl.ds(half, half), pl.ds(t, half)]))
    copies = [pltpu.make_async_copy(src, dst, sems.at[i]) for i, (src, dst) in enumerate(copies)]
    for copy in copies:
        copy.start()
    for copy in copies:
        copy.wait()


def unpack_kernel(spot_ref, *refs):
    got, (left_ref, right_ref) = refs[:-2], refs[-2:]
    half = right_ref.shape[1]
    for m, ref in enumerate(got):
        left_ref[m * half : (m + 1) * half, :] = ref[:half, :]
        right_ref[m] = ref[half:, :]


def update_kernel(spot_ref, own_ref, other_ref, left_ref, left2_ref, right_ref, *refs):
    grad, update_ref, norm_ref, root, mixed = refs
    core, lane = spot_ref[1], spot_ref[2]
    owners, chips, piece, half = own_ref.shape
    order = grad.shape[0]
    for d in range(chips):
        mine = pl.multiple_of((2 * d + core) * half, half)
        theirs = pl.multiple_of((2 * d + 1 - core) * half, half)
        grad[:, pl.ds(mine, half)] = own_ref[:, d].reshape(order, half)
        grad[:, pl.ds(theirs, half)] = other_ref[:, d].reshape(order, half)
        to = pl.ds(pl.multiple_of((lane ^ d) * half, half), half)
        for t in range(0, order, half):
            root[t : t + half, to] = right_ref[d, :, t : t + half]
    for t in range(0, order, 512):
        mixed[t : t + 512, :] = jnp.dot(grad[t : t + 512, :], root[...], preferred_element_type=F32).astype(BF16)
    total = jnp.zeros((8, 128), F32)
    count = half // piece
    for rows, which, first in ((left_ref, core, lane), (left2_ref, 1 - core, lane ^ 2)):
        part = jnp.dot(rows[...], mixed[...], preferred_element_type=F32).astype(BF16)
        wide = part.astype(F32)
        squares = jnp.sum((wide * wide).reshape(chips * half // 8, 8, chips * half), axis=0)
        for y in range(chips):
            total = total + squares[:, y * half : (y + 1) * half]
            for m in range(chips):
                block = part[m * half : (m + 1) * half, y * half : (y + 1) * half]
                spot = (first ^ m) * (2 * count) + which * count
                update_ref[pl.ds(spot, count), y] = block.reshape(count, piece, half)
    norm = jnp.sum(jnp.sum(total, axis=0, keepdims=True), axis=1, keepdims=True)
    norm_ref[...] = jnp.broadcast_to(norm, norm_ref.shape)


def product_kernel(spot_ref, grad, *refs):
    outs, (rows, columns) = refs[:-2], refs[-2:]
    core, lane = spot_ref[1], spot_ref[2]
    order = grad.shape[0]
    half = rows.shape[0] // 4
    for m in range(4):
        d = lane ^ m
        rows[m * half : (m + 1) * half, :] = grad[pl.ds(pl.multiple_of(d * 2 * half + core * half, half), half), :]
        columns[m * half : (m + 1) * half, :] = grad[:, pl.ds(pl.multiple_of((2 * d + core) * half, half), half)].T
    for n in range(0, order, 256):
        left = lax.dot_general(rows[...], grad[n : n + 256, :], (((1,), (1,)), ((), ())), preferred_element_type=F32)
        right = jnp.dot(columns[...], grad[:, n : n + 256], preferred_element_type=F32)
        for m, out in enumerate(outs):
            out[:half, n : n + 256] = left[m * half : (m + 1) * half].astype(BF16)
            out[half:, n : n + 256] = right[m * half : (m + 1) * half].astype(BF16)


def graft_kernel(spot_ref, update_ref, norm_ref, norm2_ref, adam_ref, out_ref):
    adam = jnp.sum(adam_ref[...], axis=0)
    scale = jnp.sqrt(adam / (norm_ref[0:1, :] + norm2_ref[0:1, :] + 1e-06))
    out_ref[...] = (update_ref[...].astype(F32) * scale[None, None]).astype(BF16)


def stat_kernel(side, spot_ref, p0, p1, p2, p3, stat_ref, new_ref):
    half = stat_ref.shape[1]
    for m, ref in enumerate((p0, p1, p2, p3)):

        @pl.when(pl.program_id(0) == m)
        def _():
            new_ref[0] = stat_ref[0] + ref[side * half : (side + 1) * half, :].astype(F32)


def direction_kernel(slot_ref, values_ref, out_ref, wide):
    row_blocks, rows, column_blocks, quarter = out_ref.shape
    half = quarter // 2
    size = wide.shape[0] // 2
    for b in range(row_blocks * column_blocks):
        at = spread_row(slot_ref[b])
        start = (b // column_blocks) * rows * column_blocks + b % column_blocks
        wide[pl.ds(start, rows, stride=column_blocks), :] = values_ref[at].astype(F32)
        wide[pl.ds(size + start, rows, stride=column_blocks), :] = values_ref[at + 4].astype(F32)
    for h in range(2):
        part = wide[h * size : (h + 1) * size, :].reshape(row_blocks, rows, column_blocks, half)
        out_ref[..., h * half : (h + 1) * half] = part.astype(out_ref.dtype)


def body(gradient, second_moment, stat_left, stat_right, root_left, root_right, block_slot):
    owners = lax.axis_size("fsdp")
    chips = lax.axis_size("dp")
    devices = owners * chips
    row_blocks, piece_rows, column_blocks, quarter = gradient.shape
    blocks = row_blocks * column_blocks
    order = stat_left.shape[2]
    half = quarter // 2
    core = lax.axis_index("fsdp") % 2
    chip = lax.axis_index("dp")
    spot = jnp.stack([chip, core, 2 * core + chip % 2]).astype(jnp.int32)

    def matching(m, back):
        pairs = []
        for k in range(owners // 2):
            for c in range(2):
                for d in range(chips):
                    c2, j = (d ^ m) >> 1, (d ^ m) & 1
                    here = (2 * k + c) * chips + d
                    there = (2 * k + c2) * chips + 2 * c + j
                    pairs.append((there, here) if back else (here, there))
        return pairs

    swap = [(i, i ^ 1) for i in range(owners)]

    packed = pl.pallas_call(
        pack_kernel,
        out_shape=[shape((2 * half, order), BF16)] * chips,
        in_specs=[SMEM] + [pl.BlockSpec(memory_space=pltpu.HBM)] * 2,
        out_specs=[VMEM] * chips,
        scratch_shapes=[pltpu.SemaphoreType.DMA((chips * (1 + order // half),))],
        compiler_params=pltpu.CompilerParams(vmem_limit_bytes=4 * MIB),
        cost_estimate=pl.CostEstimate(flops=0, bytes_accessed=4 * MIB, transcendentals=0),
    )(spot, root_left, root_right)
    roots = [lax.ppermute(packed[m], AXES, matching(m, False)) for m in range(chips)]

    pieces = local(
        spread_kernel, shape((devices, piece_rows, half), BF16), (block_slot, gradient),
        scratch=[pltpu.VMEM((2 * blocks * piece_rows, half), F32)], limit=6, moved=MIB * 3 // 2,
    )

    def spread(x, slots, g, second):
        x = lax.all_to_all(x, AXES, split_axis=0, concat_axis=0, tiled=True)
        new, sums = local(
            moment_kernel,
            [shape(second.shape, F32), shape((devices, 1, 128), F32)],
            (slots, g, second),
            scratch=[pltpu.VMEM((blocks, 128), F32)], limit=6, moved=MIB * 5 // 2,
        )
        return x, new, sums

    own, new_second, sent = lax.cond(
        block_slot[0] >= 0,
        spread,
        lambda x, slots, g, second: (x, second, jnp.zeros((devices, 1, 128), F32)),
        pieces, block_slot, gradient, second_moment,
    )
    adam = lax.all_to_all(sent, AXES, split_axis=0, concat_axis=0, tiled=True)

    own, *roots = lax.optimization_barrier((own, *roots))
    left, right = local(
        unpack_kernel, [shape((order // 2, order), BF16), shape((chips, half, order), BF16)], (spot, *roots),
        limit=5, moved=4 * MIB,
    )
    left2 = lax.ppermute(left, "fsdp", swap)
    other = lax.ppermute(own, "fsdp", swap)

    cut = (owners, chips, piece_rows, half)
    grad, update, norm = local(
        update_kernel,
        [shape((order, order), BF16), shape(cut, BF16), shape((8, 128), F32)],
        (spot, own.reshape(cut), other.reshape(cut), left, left2, right),
        scratch=[pltpu.VMEM((order, order // 2), BF16)] * 2,
        flops=2 * order * order * order, limit=18, moved=8 * MIB,
    )
    norm2 = lax.ppermute(norm, "fsdp", swap)
    products = local(
        product_kernel, [shape((2 * half, order), BF16)] * chips, (spot, grad),
        scratch=[pltpu.VMEM((order // 2, order), BF16)] * 2,
        flops=2 * order * order * order, limit=11, moved=4 * MIB,
    )
    update, *products = lax.optimization_barrier((update, *products))
    back = local(graft_kernel, shape(cut, BF16), (spot, update, norm, norm2, adam), limit=5, moved=2 * MIB)
    products = [lax.ppermute(products[m], AXES, matching(m, True)) for m in range(chips)]
    returned = lax.all_to_all(back.reshape(devices, piece_rows, half), AXES, split_axis=0, concat_axis=0, tiled=True)

    whole = pl.BlockSpec((2 * half, order), lambda m, s: (0, 0))
    piece = pl.BlockSpec((1, half, order), lambda m, s: ((s[0] ^ m) & 1, (s[0] ^ m) >> 1, 0))
    new_left, new_right = (
        pl.pallas_call(
            functools.partial(stat_kernel, side),
            out_shape=shape(stat.shape, F32),
            grid_spec=pltpu.PrefetchScalarGridSpec(
                num_scalar_prefetch=1, grid=(chips,), in_specs=[whole] * chips + [piece], out_specs=piece
            ),
            compiler_params=pltpu.CompilerParams(vmem_limit_bytes=8 * MIB),
            cost_estimate=pl.CostEstimate(flops=0, bytes_accessed=5 * MIB, transcendentals=0),
        )(spot, *products, stat)
        for side, stat in enumerate((stat_left, stat_right))
    )

    direction = local(
        direction_kernel, shape(gradient.shape, gradient.dtype), (block_slot, returned),
        scratch=[pltpu.VMEM((2 * blocks * piece_rows, half), F32)],
        limit=7, moved=2 * MIB,
    )
    return (new_left, new_right, new_second, direction)


def solution(mesh):
    placed = (
        P(None, "fsdp", None, "dp"),
        P(None, "fsdp", None, "dp"),
        P("fsdp", "dp", None),
        P("fsdp", "dp", None),
        P("fsdp", "dp", None),
        P("fsdp", None, "dp"),
        P(),
    )
    return jax.shard_map(
        body,
        mesh=mesh,
        in_specs=placed,
        out_specs=(
            P("fsdp", "dp", None),
            P("fsdp", "dp", None),
            P(None, "fsdp", None, "dp"),
            P(None, "fsdp", None, "dp"),
        ),
        check_vma=False,
    )
```

```python
import jax
import jax.numpy as jnp
from jax import lax
from jax.experimental import pallas as pl
from jax.experimental.pallas import tpu as pltpu
from jax.sharding import PartitionSpec as P

AXES = ("fsdp", "dp")
F32 = jnp.float32
BF16 = jnp.bfloat16
SMEM = pl.BlockSpec(memory_space=pltpu.SMEM)
VMEM = pl.BlockSpec(memory_space=pltpu.VMEM)
MIB = 1 << 20


def local(kernel, outs, inputs, scratch=(), limit=16, flops=0, moved=0):
    return pl.pallas_call(
        kernel,
        out_shape=outs,
        in_specs=[SMEM] + [VMEM] * (len(inputs) - 1),
        out_specs=jax.tree.map(lambda _: VMEM, outs),
        scratch_shapes=list(scratch),
        compiler_params=pltpu.CompilerParams(vmem_limit_bytes=limit * MIB),
        cost_estimate=pl.CostEstimate(flops=flops, bytes_accessed=moved, transcendentals=0),
    )(*inputs)


def shape(dims, dtype):
    return jax.ShapeDtypeStruct(dims, dtype)


def spread_row(slot):
    return ((slot >> 2) << 3) + (slot & 3)


def spread_kernel(slot_ref, grad_ref, out_ref, wide):
    row_blocks, rows, column_blocks, quarter = grad_ref.shape
    half = quarter // 2
    out_ref[...] = jnp.zeros_like(out_ref)
    size = wide.shape[0] // 2
    for h in range(2):
        wide[h * size : (h + 1) * size, :] = grad_ref[..., h * half : (h + 1) * half].astype(F32).reshape(size, half)
    for b in range(row_blocks * column_blocks):
        start = (b // column_blocks) * rows * column_blocks + b % column_blocks
        at = spread_row(slot_ref[b])
        out_ref[at] = wide[pl.ds(start, rows, stride=column_blocks), :].astype(BF16)
        out_ref[at + 4] = wide[pl.ds(size + start, rows, stride=column_blocks), :].astype(BF16)


def moment_kernel(slot_ref, grad_ref, second_ref, new_ref, sent_ref, part):
    row_blocks, _, column_blocks, _ = grad_ref.shape
    sent_ref[...] = jnp.zeros_like(sent_ref)
    for r in range(row_blocks):
        g = grad_ref[r].astype(F32)
        new = 0.9 * second_ref[r] + 0.1 * g * g
        new_ref[r] = new
        adam = g / (jnp.sqrt(new) + 1e-08)
        sums = jnp.sum(jnp.sum(adam * adam, axis=0), axis=1, keepdims=True)
        part[r * column_blocks : (r + 1) * column_blocks, :] = jnp.broadcast_to(sums, (column_blocks, 128))
    owner = lax.broadcasted_iota(jnp.int32, (1, 128), 1) >> 5
    for b in range(row_blocks * column_blocks):
        slot = slot_ref[b]
        at = (slot >> 2) * 2
        row = sent_ref[at] + jnp.where(owner == (slot & 3), part[b : b + 1, :], 0.0)
        sent_ref[at] = row
        sent_ref[at + 1] = row


def pack_kernel(spot_ref, left_ref, right_ref, *refs):
    outs, sems = refs[:-1], refs[-1]
    half = left_ref.shape[1] // 2
    order = left_ref.shape[2]
    copies = []
    for m, out in enumerate(outs):
        to = spot_ref[0] ^ m
        part = pl.ds(pl.multiple_of((to >> 1) * half, half), half)
        copies.append((left_ref.at[to & 1, part], out.at[pl.ds(0, half)]))
        for t in range(0, order, half):
            copies.append((right_ref.at[to & 1, pl.ds(t, half), part], out.at[pl.ds(half, half), pl.ds(t, half)]))
    copies = [pltpu.make_async_copy(src, dst, sems.at[i]) for i, (src, dst) in enumerate(copies)]
    for copy in copies:
        copy.start()
    for copy in copies:
        copy.wait()


def unpack_kernel(spot_ref, *refs):
    got, (left_ref, right_ref) = refs[:-2], refs[-2:]
    half = right_ref.shape[1]
    for m, ref in enumerate(got):
        left_ref[m * half : (m + 1) * half, :] = ref[:half, :]
        right_ref[m] = ref[half:, :]


def update_kernel(spot_ref, own_ref, other_ref, left_ref, left2_ref, right_ref, *refs):
    grad, update_ref, norm_ref, root, mixed = refs
    core, lane = spot_ref[1], spot_ref[2]
    owners, chips, piece, half = own_ref.shape
    order = grad.shape[0]
    for d in range(chips):
        mine = pl.multiple_of((2 * d + core) * half, half)
        theirs = pl.multiple_of((2 * d + 1 - core) * half, half)
        grad[:, pl.ds(mine, half)] = own_ref[:, d].reshape(order, half)
        grad[:, pl.ds(theirs, half)] = other_ref[:, d].reshape(order, half)
        to = pl.ds(pl.multiple_of((lane ^ d) * half, half), half)
        for t in range(0, order, half):
            root[t : t + half, to] = right_ref[d, :, t : t + half]
    for t in range(0, order, 512):
        mixed[t : t + 512, :] = jnp.dot(grad[t : t + 512, :], root[...], preferred_element_type=F32).astype(BF16)
    total = jnp.zeros((8, 128), F32)
    count = half // piece
    for rows, which, first in ((left_ref, core, lane), (left2_ref, 1 - core, lane ^ 2)):
        part = jnp.dot(rows[...], mixed[...], preferred_element_type=F32).astype(BF16)
        wide = part.astype(F32)
        squares = jnp.sum((wide * wide).reshape(chips * half // 8, 8, chips * half), axis=0)
        for y in range(chips):
            total = total + squares[:, y * half : (y + 1) * half]
            for m in range(chips):
                block = part[m * half : (m + 1) * half, y * half : (y + 1) * half]
                spot = (first ^ m) * (2 * count) + which * count
                update_ref[pl.ds(spot, count), y] = block.reshape(count, piece, half)
    norm = jnp.sum(jnp.sum(total, axis=0, keepdims=True), axis=1, keepdims=True)
    norm_ref[...] = jnp.broadcast_to(norm, norm_ref.shape)


def product_kernel(spot_ref, grad, *refs):
    outs, (rows, columns) = refs[:-2], refs[-2:]
    core, lane = spot_ref[1], spot_ref[2]
    order = grad.shape[0]
    half = rows.shape[0] // 4
    for m in range(4):
        d = lane ^ m
        rows[m * half : (m + 1) * half, :] = grad[pl.ds(pl.multiple_of(d * 2 * half + core * half, half), half), :]
        columns[m * half : (m + 1) * half, :] = grad[:, pl.ds(pl.multiple_of((2 * d + core) * half, half), half)].T
    for n in range(0, order, 256):
        left = lax.dot_general(rows[...], grad[n : n + 256, :], (((1,), (1,)), ((), ())), preferred_element_type=F32)
        right = jnp.dot(columns[...], grad[:, n : n + 256], preferred_element_type=F32)
        for m, out in enumerate(outs):
            out[:half, n : n + 256] = left[m * half : (m + 1) * half].astype(BF16)
            out[half:, n : n + 256] = right[m * half : (m + 1) * half].astype(BF16)


def graft_kernel(spot_ref, update_ref, norm_ref, norm2_ref, adam0, adam1, adam2, adam3, out_ref):
    adam = adam0[...] + adam1[...] + adam2[...] + adam3[...]
    owner = lax.broadcasted_iota(jnp.int32, (1, 128), 1) >> 5
    adam = jnp.max(jnp.where(owner == spot_ref[0], adam, 0.0), axis=1, keepdims=True)
    scale = jnp.sqrt(adam / (norm_ref[0:1, :] + norm2_ref[0:1, :] + 1e-06))
    out_ref[...] = (update_ref[...].astype(F32) * scale[None, None]).astype(BF16)


def stat_kernel(spot_ref, p0, p1, p2, p3, left_ref, right_ref, new_left_ref, new_right_ref):
    half = left_ref.shape[1]
    for m, ref in enumerate((p0, p1, p2, p3)):

        @pl.when(pl.program_id(0) == m)
        def _():
            new_left_ref[0] = left_ref[0] + ref[:half, :].astype(F32)
            new_right_ref[0] = right_ref[0] + ref[half:, :].astype(F32)


def direction_kernel(slot_ref, values_ref, out_ref, wide):
    row_blocks, rows, column_blocks, quarter = out_ref.shape
    half = quarter // 2
    size = wide.shape[0] // 2
    for b in range(row_blocks * column_blocks):
        at = spread_row(slot_ref[b])
        start = (b // column_blocks) * rows * column_blocks + b % column_blocks
        wide[pl.ds(start, rows, stride=column_blocks), :] = values_ref[at].astype(F32)
        wide[pl.ds(size + start, rows, stride=column_blocks), :] = values_ref[at + 4].astype(F32)
    for h in range(2):
        part = wide[h * size : (h + 1) * size, :].reshape(row_blocks, rows, column_blocks, half)
        out_ref[..., h * half : (h + 1) * half] = part.astype(out_ref.dtype)


def body(gradient, second_moment, stat_left, stat_right, root_left, root_right, block_slot):
    owners = lax.axis_size("fsdp")
    chips = lax.axis_size("dp")
    devices = owners * chips
    row_blocks, piece_rows, column_blocks, quarter = gradient.shape
    blocks = row_blocks * column_blocks
    order = stat_left.shape[2]
    half = quarter // 2
    core = lax.axis_index("fsdp") % 2
    chip = lax.axis_index("dp")
    spot = jnp.stack([chip, core, 2 * core + chip % 2]).astype(jnp.int32)

    def matching(m, back):
        pairs = []
        for k in range(owners // 2):
            for c in range(2):
                for d in range(chips):
                    c2, j = (d ^ m) >> 1, (d ^ m) & 1
                    here = (2 * k + c) * chips + d
                    there = (2 * k + c2) * chips + 2 * c + j
                    pairs.append((there, here) if back else (here, there))
        return pairs

    swap = [(i, i ^ 1) for i in range(owners)]

    packed = pl.pallas_call(
        pack_kernel,
        out_shape=[shape((2 * half, order), BF16)] * chips,
        in_specs=[SMEM] + [pl.BlockSpec(memory_space=pl.ANY)] * 2,
        out_specs=[VMEM] * chips,
        scratch_shapes=[pltpu.SemaphoreType.DMA((chips * (1 + order // half),))],
        compiler_params=pltpu.CompilerParams(vmem_limit_bytes=4 * MIB),
        cost_estimate=pl.CostEstimate(flops=0, bytes_accessed=4 * MIB, transcendentals=0),
    )(spot, root_left, root_right)
    roots = [lax.ppermute(packed[m], AXES, matching(m, False)) for m in range(chips)]

    new_second, sent = local(
        moment_kernel,
        [shape(second_moment.shape, F32), shape((owners, 1, 128), F32)],
        (block_slot, gradient, second_moment),
        scratch=[pltpu.VMEM((blocks, 128), F32)], limit=6, moved=MIB * 5 // 2,
    )
    adam = lax.all_to_all(sent, "fsdp", split_axis=0, concat_axis=0, tiled=True)

    pieces = local(
        spread_kernel, shape((devices, piece_rows, half), BF16), (block_slot, gradient),
        scratch=[pltpu.VMEM((2 * blocks * piece_rows, half), F32)], limit=6, moved=MIB * 3 // 2,
    )
    own = lax.cond(
        block_slot[0] >= 0,
        lambda x: lax.all_to_all(x, AXES, split_axis=0, concat_axis=0, tiled=True),
        lambda x: x,
        pieces,
    )

    own, *roots = lax.optimization_barrier((own, *roots))
    left, right = local(
        unpack_kernel, [shape((order // 2, order), BF16), shape((chips, half, order), BF16)], (spot, *roots),
        limit=5, moved=4 * MIB,
    )
    left2 = lax.ppermute(left, "fsdp", swap)
    other = lax.ppermute(own, "fsdp", swap)

    cut = (owners, chips, piece_rows, half)
    grad, update, norm = local(
        update_kernel,
        [shape((order, order), BF16), shape(cut, BF16), shape((8, 128), F32)],
        (spot, own.reshape(cut), other.reshape(cut), left, left2, right),
        scratch=[pltpu.VMEM((order, order // 2), BF16)] * 2,
        flops=2 * order * order * order, limit=18, moved=8 * MIB,
    )
    norm, adam = lax.optimization_barrier((norm, adam))
    norm2 = lax.ppermute(norm, "fsdp", swap)
    adam = adam.sum(axis=0)
    adams = [adam] + [lax.ppermute(adam, "dp", [(i, (i + k) % chips) for i in range(chips)]) for k in range(1, chips)]
    products = local(
        product_kernel, [shape((2 * half, order), BF16)] * chips, (spot, grad),
        scratch=[pltpu.VMEM((order // 2, order), BF16)] * 2,
        flops=2 * order * order * order, limit=11, moved=4 * MIB,
    )
    update, *products = lax.optimization_barrier((update, *products))
    back = local(graft_kernel, shape(cut, BF16), (spot, update, norm, norm2, *adams), limit=5, moved=2 * MIB)
    products = [lax.ppermute(products[m], AXES, matching(m, True)) for m in range(chips)]
    returned = lax.all_to_all(back.reshape(devices, piece_rows, half), AXES, split_axis=0, concat_axis=0, tiled=True)

    whole = pl.BlockSpec((2 * half, order), lambda m, s: (0, 0))
    piece = pl.BlockSpec((1, half, order), lambda m, s: ((s[0] ^ m) & 1, (s[0] ^ m) >> 1, 0))
    new_left, new_right = pl.pallas_call(
        stat_kernel,
        out_shape=[shape(stat_left.shape, F32), shape(stat_right.shape, F32)],
        grid_spec=pltpu.PrefetchScalarGridSpec(
            num_scalar_prefetch=1, grid=(chips,), in_specs=[whole] * chips + [piece] * 2, out_specs=[piece] * 2
        ),
        compiler_params=pltpu.CompilerParams(vmem_limit_bytes=10 * MIB),
        cost_estimate=pl.CostEstimate(flops=0, bytes_accessed=10 * MIB, transcendentals=0),
    )(spot, *products, stat_left, stat_right)

    direction = local(
        direction_kernel, shape(gradient.shape, gradient.dtype), (block_slot, returned),
        scratch=[pltpu.VMEM((2 * blocks * piece_rows, half), F32)],
        limit=7, moved=2 * MIB,
    )
    return (new_left, new_right, new_second, direction)


def solution(mesh):
    placed = (
        P(None, "fsdp", None, "dp"),
        P(None, "fsdp", None, "dp"),
        P("fsdp", "dp", None),
        P("fsdp", "dp", None),
        P("fsdp", "dp", None),
        P("fsdp", None, "dp"),
        P(),
    )
    return jax.shard_map(
        body,
        mesh=mesh,
        in_specs=placed,
        out_specs=(
            P("fsdp", "dp", None),
            P("fsdp", "dp", None),
            P(None, "fsdp", None, "dp"),
            P(None, "fsdp", None, "dp"),
        ),
        check_vma=False,
    )
```

```python
import jax
import jax.numpy as jnp
from jax import lax
from jax.experimental import pallas as pl
from jax.experimental.pallas import tpu as pltpu
from jax.sharding import PartitionSpec as P

AXES = ("fsdp", "dp")
F32 = jnp.float32
BF16 = jnp.bfloat16
SMEM = pl.BlockSpec(memory_space=pltpu.SMEM)
VMEM = pl.BlockSpec(memory_space=pltpu.VMEM)
MIB = 1 << 20


def local(kernel, outs, inputs, scratch=(), limit=16, flops=0, moved=0):
    return pl.pallas_call(
        kernel,
        out_shape=outs,
        in_specs=[SMEM] + [VMEM] * (len(inputs) - 1),
        out_specs=jax.tree.map(lambda _: VMEM, outs),
        scratch_shapes=list(scratch),
        compiler_params=pltpu.CompilerParams(vmem_limit_bytes=limit * MIB),
        cost_estimate=pl.CostEstimate(flops=flops, bytes_accessed=moved, transcendentals=0),
    )(*inputs)


def shape(dims, dtype):
    return jax.ShapeDtypeStruct(dims, dtype)


def spread_row(slot):
    return ((slot >> 2) << 3) + (slot & 3)


def spread_kernel(slot_ref, grad_ref, out_ref, wide):
    row_blocks, rows, column_blocks, quarter = grad_ref.shape
    half = quarter // 2
    out_ref[...] = jnp.zeros_like(out_ref)
    size = wide.shape[0] // 2
    for h in range(2):
        wide[h * size : (h + 1) * size, :] = grad_ref[..., h * half : (h + 1) * half].astype(F32).reshape(size, half)
    for b in range(row_blocks * column_blocks):
        start = (b // column_blocks) * rows * column_blocks + b % column_blocks
        at = spread_row(slot_ref[b])
        out_ref[at] = wide[pl.ds(start, rows, stride=column_blocks), :].astype(BF16)
        out_ref[at + 4] = wide[pl.ds(size + start, rows, stride=column_blocks), :].astype(BF16)


def moment_kernel(slot_ref, grad_ref, second_ref, new_ref, sent_ref, part):
    row_blocks, _, column_blocks, _ = grad_ref.shape
    sent_ref[...] = jnp.zeros_like(sent_ref)
    for r in range(row_blocks):
        g = grad_ref[r].astype(F32)
        new = 0.9 * second_ref[r] + 0.1 * g * g
        new_ref[r] = new
        adam = g / (jnp.sqrt(new) + 1e-08)
        sums = jnp.sum(jnp.sum(adam * adam, axis=0), axis=1, keepdims=True)
        part[r * column_blocks : (r + 1) * column_blocks, :] = jnp.broadcast_to(sums, (column_blocks, 128))
    for b in range(row_blocks * column_blocks):
        at = spread_row(slot_ref[b])
        sent_ref[at] = part[b : b + 1, :]
        sent_ref[at + 4] = part[b : b + 1, :]


def pack_kernel(spot_ref, left_ref, right_ref, *refs):
    outs, sems = refs[:-1], refs[-1]
    half = left_ref.shape[1] // 2
    order = left_ref.shape[2]
    copies = []
    for m, out in enumerate(outs):
        to = spot_ref[0] ^ m
        part = pl.ds(pl.multiple_of((to >> 1) * half, half), half)
        copies.append((left_ref.at[to & 1, part], out.at[pl.ds(0, half)]))
        for t in range(0, order, half):
            copies.append((right_ref.at[to & 1, pl.ds(t, half), part], out.at[pl.ds(half, half), pl.ds(t, half)]))
    copies = [pltpu.make_async_copy(src, dst, sems.at[i]) for i, (src, dst) in enumerate(copies)]
    for copy in copies:
        copy.start()
    for copy in copies:
        copy.wait()


def unpack_kernel(spot_ref, *refs):
    got, (left_ref, right_ref) = refs[:-2], refs[-2:]
    half = right_ref.shape[1]
    for m, ref in enumerate(got):
        left_ref[m * half : (m + 1) * half, :] = ref[:half, :]
        right_ref[m] = ref[half:, :]


def update_kernel(spot_ref, own_ref, other_ref, left_ref, left2_ref, right_ref, *refs):
    grad, update_ref, norm_ref, root, mixed = refs
    core, lane = spot_ref[1], spot_ref[2]
    owners, chips, piece, half = own_ref.shape
    order = grad.shape[0]
    for d in range(chips):
        mine = pl.multiple_of((2 * d + core) * half, half)
        theirs = pl.multiple_of((2 * d + 1 - core) * half, half)
        grad[:, pl.ds(mine, half)] = own_ref[:, d].reshape(order, half)
        grad[:, pl.ds(theirs, half)] = other_ref[:, d].reshape(order, half)
        to = pl.ds(pl.multiple_of((lane ^ d) * half, half), half)
        for t in range(0, order, half):
            root[t : t + half, to] = right_ref[d, :, t : t + half]
    for t in range(0, order, 512):
        mixed[t : t + 512, :] = jnp.dot(grad[t : t + 512, :], root[...], preferred_element_type=F32).astype(BF16)
    total = jnp.zeros((8, 128), F32)
    count = half // piece
    for rows, which, first in ((left_ref, core, lane), (left2_ref, 1 - core, lane ^ 2)):
        part = jnp.dot(rows[...], mixed[...], preferred_element_type=F32).astype(BF16)
        wide = part.astype(F32)
        squares = jnp.sum((wide * wide).reshape(chips * half // 8, 8, chips * half), axis=0)
        for y in range(chips):
            total = total + squares[:, y * half : (y + 1) * half]
            for m in range(chips):
                block = part[m * half : (m + 1) * half, y * half : (y + 1) * half]
                spot = (first ^ m) * (2 * count) + which * count
                update_ref[pl.ds(spot, count), y] = block.reshape(count, piece, half)
    norm = jnp.sum(jnp.sum(total, axis=0, keepdims=True), axis=1, keepdims=True)
    norm_ref[...] = jnp.broadcast_to(norm, norm_ref.shape)


def product_kernel(spot_ref, grad, *refs):
    outs, (rows, columns) = refs[:-2], refs[-2:]
    core, lane = spot_ref[1], spot_ref[2]
    order = grad.shape[0]
    half = rows.shape[0] // 4
    for m in range(4):
        d = lane ^ m
        rows[m * half : (m + 1) * half, :] = grad[pl.ds(pl.multiple_of(d * 2 * half + core * half, half), half), :]
        columns[m * half : (m + 1) * half, :] = grad[:, pl.ds(pl.multiple_of((2 * d + core) * half, half), half)].T
    for n in range(0, order, 256):
        left = lax.dot_general(rows[...], grad[n : n + 256, :], (((1,), (1,)), ((), ())), preferred_element_type=F32)
        right = jnp.dot(columns[...], grad[:, n : n + 256], preferred_element_type=F32)
        for m, out in enumerate(outs):
            out[:half, n : n + 256] = left[m * half : (m + 1) * half].astype(BF16)
            out[half:, n : n + 256] = right[m * half : (m + 1) * half].astype(BF16)


def graft_kernel(spot_ref, update_ref, norm_ref, norm2_ref, adam_ref, out_ref):
    adam = jnp.sum(adam_ref[...], axis=0)
    scale = jnp.sqrt(adam / (norm_ref[0:1, :] + norm2_ref[0:1, :] + 1e-06))
    out_ref[...] = (update_ref[...].astype(F32) * scale[None, None]).astype(BF16)


def stat_kernel(spot_ref, p0, p1, p2, p3, left_ref, right_ref, new_left_ref, new_right_ref):
    half = left_ref.shape[1]
    for m, ref in enumerate((p0, p1, p2, p3)):

        @pl.when(pl.program_id(0) == m)
        def _():
            new_left_ref[0] = left_ref[0] + ref[:half, :].astype(F32)
            new_right_ref[0] = right_ref[0] + ref[half:, :].astype(F32)


def direction_kernel(slot_ref, values_ref, out_ref, wide):
    row_blocks, rows, column_blocks, quarter = out_ref.shape
    half = quarter // 2
    size = wide.shape[0] // 2
    for b in range(row_blocks * column_blocks):
        at = spread_row(slot_ref[b])
        start = (b // column_blocks) * rows * column_blocks + b % column_blocks
        wide[pl.ds(start, rows, stride=column_blocks), :] = values_ref[at].astype(F32)
        wide[pl.ds(size + start, rows, stride=column_blocks), :] = values_ref[at + 4].astype(F32)
    for h in range(2):
        part = wide[h * size : (h + 1) * size, :].reshape(row_blocks, rows, column_blocks, half)
        out_ref[..., h * half : (h + 1) * half] = part.astype(out_ref.dtype)


def body(gradient, second_moment, stat_left, stat_right, root_left, root_right, block_slot):
    owners = lax.axis_size("fsdp")
    chips = lax.axis_size("dp")
    devices = owners * chips
    row_blocks, piece_rows, column_blocks, quarter = gradient.shape
    blocks = row_blocks * column_blocks
    order = stat_left.shape[2]
    half = quarter // 2
    core = lax.axis_index("fsdp") % 2
    chip = lax.axis_index("dp")
    spot = jnp.stack([chip, core, 2 * core + chip % 2]).astype(jnp.int32)

    def matching(m, back):
        pairs = []
        for k in range(owners // 2):
            for c in range(2):
                for d in range(chips):
                    c2, j = (d ^ m) >> 1, (d ^ m) & 1
                    here = (2 * k + c) * chips + d
                    there = (2 * k + c2) * chips + 2 * c + j
                    pairs.append((there, here) if back else (here, there))
        return pairs

    swap = [(i, i ^ 1) for i in range(owners)]

    packed = pl.pallas_call(
        pack_kernel,
        out_shape=[shape((2 * half, order), BF16)] * chips,
        in_specs=[SMEM] + [pl.BlockSpec(memory_space=pl.ANY)] * 2,
        out_specs=[VMEM] * chips,
        scratch_shapes=[pltpu.SemaphoreType.DMA((chips * (1 + order // half),))],
        compiler_params=pltpu.CompilerParams(vmem_limit_bytes=4 * MIB),
        cost_estimate=pl.CostEstimate(flops=0, bytes_accessed=4 * MIB, transcendentals=0),
    )(spot, root_left, root_right)
    roots = [lax.ppermute(packed[m], AXES, matching(m, False)) for m in range(chips)]

    pieces = local(
        spread_kernel, shape((devices, piece_rows, half), BF16), (block_slot, gradient),
        scratch=[pltpu.VMEM((2 * blocks * piece_rows, half), F32)], limit=6, moved=MIB * 3 // 2,
    )

    def spread(x, slots, g, second):
        x = lax.all_to_all(x, AXES, split_axis=0, concat_axis=0, tiled=True)
        new, sums = local(
            moment_kernel,
            [shape(second.shape, F32), shape((devices, 1, 128), F32)],
            (slots, g, second),
            scratch=[pltpu.VMEM((blocks, 128), F32)], limit=6, moved=MIB * 5 // 2,
        )
        return x, new, sums

    own, new_second, sent = lax.cond(
        block_slot[0] >= 0,
        spread,
        lambda x, slots, g, second: (jnp.zeros_like(x), jnp.zeros_like(second), jnp.zeros((devices, 1, 128), F32)),
        pieces, block_slot, gradient, second_moment,
    )
    adam = lax.all_to_all(sent, AXES, split_axis=0, concat_axis=0, tiled=True)

    own, *roots = lax.optimization_barrier((own, *roots))
    left, right = local(
        unpack_kernel, [shape((order // 2, order), BF16), shape((chips, half, order), BF16)], (spot, *roots),
        limit=5, moved=4 * MIB,
    )
    left2 = lax.ppermute(left, "fsdp", swap)
    other = lax.ppermute(own, "fsdp", swap)

    cut = (owners, chips, piece_rows, half)
    grad, update, norm = local(
        update_kernel,
        [shape((order, order), BF16), shape(cut, BF16), shape((8, 128), F32)],
        (spot, own.reshape(cut), other.reshape(cut), left, left2, right),
        scratch=[pltpu.VMEM((order, order // 2), BF16)] * 2,
        flops=2 * order * order * order, limit=18, moved=8 * MIB,
    )
    norm2 = lax.ppermute(norm, "fsdp", swap)
    products = local(
        product_kernel, [shape((2 * half, order), BF16)] * chips, (spot, grad),
        scratch=[pltpu.VMEM((order // 2, order), BF16)] * 2,
        flops=2 * order * order * order, limit=11, moved=4 * MIB,
    )
    update, *products = lax.optimization_barrier((update, *products))
    back = local(graft_kernel, shape(cut, BF16), (spot, update, norm, norm2, adam), limit=5, moved=2 * MIB)
    products = [lax.ppermute(products[m], AXES, matching(m, True)) for m in range(chips)]
    returned = lax.all_to_all(back.reshape(devices, piece_rows, half), AXES, split_axis=0, concat_axis=0, tiled=True)

    whole = pl.BlockSpec((2 * half, order), lambda m, s: (0, 0))
    piece = pl.BlockSpec((1, half, order), lambda m, s: ((s[0] ^ m) & 1, (s[0] ^ m) >> 1, 0))
    new_left, new_right = pl.pallas_call(
        stat_kernel,
        out_shape=[shape(stat_left.shape, F32), shape(stat_right.shape, F32)],
        grid_spec=pltpu.PrefetchScalarGridSpec(
            num_scalar_prefetch=1, grid=(chips,), in_specs=[whole] * chips + [piece] * 2, out_specs=[piece] * 2
        ),
        compiler_params=pltpu.CompilerParams(vmem_limit_bytes=10 * MIB),
        cost_estimate=pl.CostEstimate(flops=0, bytes_accessed=10 * MIB, transcendentals=0),
    )(spot, *products, stat_left, stat_right)

    direction = local(
        direction_kernel, shape(gradient.shape, gradient.dtype), (block_slot, returned),
        scratch=[pltpu.VMEM((2 * blocks * piece_rows, half), F32)],
        limit=7, moved=2 * MIB,
    )
    return (new_left, new_right, new_second, direction)


def solution(mesh):
    placed = (
        P(None, "fsdp", None, "dp"),
        P(None, "fsdp", None, "dp"),
        P("fsdp", "dp", None),
        P("fsdp", "dp", None),
        P("fsdp", "dp", None),
        P("fsdp", None, "dp"),
        P(),
    )
    return jax.shard_map(
        body,
        mesh=mesh,
        in_specs=placed,
        out_specs=(
            P("fsdp", "dp", None),
            P("fsdp", "dp", None),
            P(None, "fsdp", None, "dp"),
            P(None, "fsdp", None, "dp"),
        ),
        check_vma=False,
    )
```

```python
import jax
import jax.numpy as jnp
from jax import lax
from jax.experimental import pallas as pl
from jax.experimental.pallas import tpu as pltpu
from jax.sharding import PartitionSpec as P

AXES = ("fsdp", "dp")
F32 = jnp.float32
BF16 = jnp.bfloat16
SMEM = pl.BlockSpec(memory_space=pltpu.SMEM)
VMEM = pl.BlockSpec(memory_space=pltpu.VMEM)
MIB = 1 << 20


def local(kernel, outs, inputs, scratch=(), limit=16, flops=0, moved=0):
    return pl.pallas_call(
        kernel,
        out_shape=outs,
        in_specs=[SMEM] + [VMEM] * (len(inputs) - 1),
        out_specs=jax.tree.map(lambda _: VMEM, outs),
        scratch_shapes=list(scratch),
        compiler_params=pltpu.CompilerParams(vmem_limit_bytes=limit * MIB),
        cost_estimate=pl.CostEstimate(flops=flops, bytes_accessed=moved, transcendentals=0),
    )(*inputs)


def shape(dims, dtype):
    return jax.ShapeDtypeStruct(dims, dtype)


def spread_row(slot):
    return ((slot >> 2) << 3) + (slot & 3)


def spread_kernel(slot_ref, grad_ref, out_ref, wide):
    row_blocks, rows, column_blocks, quarter = grad_ref.shape
    half = quarter // 2
    out_ref[...] = jnp.zeros_like(out_ref)
    size = wide.shape[0] // 2
    for h in range(2):
        wide[h * size : (h + 1) * size, :] = grad_ref[..., h * half : (h + 1) * half].astype(F32).reshape(size, half)
    for b in range(row_blocks * column_blocks):
        start = (b // column_blocks) * rows * column_blocks + b % column_blocks
        at = spread_row(slot_ref[b])
        out_ref[at] = wide[pl.ds(start, rows, stride=column_blocks), :].astype(BF16)
        out_ref[at + 4] = wide[pl.ds(size + start, rows, stride=column_blocks), :].astype(BF16)


def moment_kernel(slot_ref, grad_ref, second_ref, new_ref, sent_ref, part):
    row_blocks, _, column_blocks, _ = grad_ref.shape
    sent_ref[...] = jnp.zeros_like(sent_ref)
    for r in range(row_blocks):
        g = grad_ref[r].astype(F32)
        new = 0.9 * second_ref[r] + 0.1 * g * g
        new_ref[r] = new
        adam = g / (jnp.sqrt(new) + 1e-08)
        sums = jnp.sum(jnp.sum(adam * adam, axis=0), axis=1, keepdims=True)
        part[r * column_blocks : (r + 1) * column_blocks, :] = jnp.broadcast_to(sums, (column_blocks, 128))
    for b in range(row_blocks * column_blocks):
        at = spread_row(slot_ref[b])
        sent_ref[at] = part[b : b + 1, :]
        sent_ref[at + 4] = part[b : b + 1, :]


def pack_kernel(spot_ref, left_ref, right_ref, *refs):
    outs, sems = refs[:-1], refs[-1]
    half = left_ref.shape[1] // 2
    order = left_ref.shape[2]
    copies = []
    for m, out in enumerate(outs):
        to = spot_ref[0] ^ m
        part = pl.ds(pl.multiple_of((to >> 1) * half, half), half)
        copies.append((left_ref.at[to & 1, part], out.at[pl.ds(0, half)]))
        for t in range(0, order, half):
            copies.append((right_ref.at[to & 1, pl.ds(t, half), part], out.at[pl.ds(half, half), pl.ds(t, half)]))
    copies = [pltpu.make_async_copy(src, dst, sems.at[i]) for i, (src, dst) in enumerate(copies)]
    for copy in copies:
        copy.start()
    for copy in copies:
        copy.wait()


def unpack_kernel(spot_ref, *refs):
    got, (left_ref, right_ref) = refs[:-2], refs[-2:]
    half = right_ref.shape[1]
    for m, ref in enumerate(got):
        left_ref[m * half : (m + 1) * half, :] = ref[:half, :]
        right_ref[m] = ref[half:, :]


def update_kernel(spot_ref, own_ref, other_ref, left_ref, left2_ref, right_ref, *refs):
    grad, update_ref, norm_ref, root, mixed = refs
    core, lane = spot_ref[1], spot_ref[2]
    owners, chips, piece, half = own_ref.shape
    order = grad.shape[0]
    for d in range(chips):
        mine = pl.multiple_of((2 * d + core) * half, half)
        theirs = pl.multiple_of((2 * d + 1 - core) * half, half)
        grad[:, pl.ds(mine, half)] = own_ref[:, d].reshape(order, half)
        grad[:, pl.ds(theirs, half)] = other_ref[:, d].reshape(order, half)
        to = pl.ds(pl.multiple_of((lane ^ d) * half, half), half)
        for t in range(0, order, half):
            root[t : t + half, to] = right_ref[d, :, t : t + half]
    for t in range(0, order, 512):
        mixed[t : t + 512, :] = jnp.dot(grad[t : t + 512, :], root[...], preferred_element_type=F32).astype(BF16)
    total = jnp.zeros((8, 128), F32)
    count = half // piece
    for rows, which, first in ((left_ref, core, lane), (left2_ref, 1 - core, lane ^ 2)):
        part = jnp.dot(rows[...], mixed[...], preferred_element_type=F32).astype(BF16)
        wide = part.astype(F32)
        squares = jnp.sum((wide * wide).reshape(chips * half // 8, 8, chips * half), axis=0)
        for y in range(chips):
            total = total + squares[:, y * half : (y + 1) * half]
            for m in range(chips):
                block = part[m * half : (m + 1) * half, y * half : (y + 1) * half]
                spot = (first ^ m) * (2 * count) + which * count
                update_ref[pl.ds(spot, count), y] = block.reshape(count, piece, half)
    norm = jnp.sum(jnp.sum(total, axis=0, keepdims=True), axis=1, keepdims=True)
    norm_ref[...] = jnp.broadcast_to(norm, norm_ref.shape)


def product_kernel(spot_ref, grad, *refs):
    outs, (rows, columns) = refs[:-2], refs[-2:]
    core, lane = spot_ref[1], spot_ref[2]
    order = grad.shape[0]
    half = rows.shape[0] // 4
    for m in range(4):
        d = lane ^ m
        rows[m * half : (m + 1) * half, :] = grad[pl.ds(pl.multiple_of(d * 2 * half + core * half, half), half), :]
        columns[m * half : (m + 1) * half, :] = grad[:, pl.ds(pl.multiple_of((2 * d + core) * half, half), half)].T
    for n in range(0, order, 256):
        left = lax.dot_general(rows[...], grad[n : n + 256, :], (((1,), (1,)), ((), ())), preferred_element_type=F32)
        right = jnp.dot(columns[...], grad[:, n : n + 256], preferred_element_type=F32)
        for m, out in enumerate(outs):
            out[:half, n : n + 256] = left[m * half : (m + 1) * half].astype(BF16)
            out[half:, n : n + 256] = right[m * half : (m + 1) * half].astype(BF16)


def graft_kernel(spot_ref, update_ref, norm_ref, norm2_ref, adam_ref, out_ref):
    adam = jnp.sum(adam_ref[...], axis=0)
    scale = jnp.sqrt(adam / (norm_ref[0:1, :] + norm2_ref[0:1, :] + 1e-06))
    out_ref[...] = (update_ref[...].astype(F32) * scale[None, None]).astype(BF16)


def stat_kernel(spot_ref, p0, p1, p2, p3, left_ref, right_ref, new_left_ref, new_right_ref, held, sems):
    half = held.shape[1]
    moves = []
    for m, ref in enumerate((p0, p1, p2, p3)):
        to = spot_ref[0] ^ m
        part = pl.ds(pl.multiple_of((to >> 1) * half, half), half)
        for side, (old, new) in enumerate(((left_ref, new_left_ref), (right_ref, new_right_ref))):
            i = 2 * m + side
            moves.append((
                pltpu.make_async_copy(old.at[to & 1, part], held.at[i], sems.at[0, i]),
                ref.at[pl.ds(side * half, half)],
                pltpu.make_async_copy(held.at[i], new.at[to & 1, part], sems.at[1, i]),
            ))
    for read, _, _ in moves:
        read.start()
    for i, (read, term, write) in enumerate(moves):
        read.wait()
        held[i] = held[i] + term[...].astype(F32)
        write.start()
    for _, _, write in moves:
        write.wait()


def direction_kernel(slot_ref, values_ref, out_ref, wide):
    row_blocks, rows, column_blocks, quarter = out_ref.shape
    half = quarter // 2
    size = wide.shape[0] // 2
    for b in range(row_blocks * column_blocks):
        at = spread_row(slot_ref[b])
        start = (b // column_blocks) * rows * column_blocks + b % column_blocks
        wide[pl.ds(start, rows, stride=column_blocks), :] = values_ref[at].astype(F32)
        wide[pl.ds(size + start, rows, stride=column_blocks), :] = values_ref[at + 4].astype(F32)
    for h in range(2):
        part = wide[h * size : (h + 1) * size, :].reshape(row_blocks, rows, column_blocks, half)
        out_ref[..., h * half : (h + 1) * half] = part.astype(out_ref.dtype)


def body(gradient, second_moment, stat_left, stat_right, root_left, root_right, block_slot):
    owners = lax.axis_size("fsdp")
    chips = lax.axis_size("dp")
    devices = owners * chips
    row_blocks, piece_rows, column_blocks, quarter = gradient.shape
    blocks = row_blocks * column_blocks
    order = stat_left.shape[2]
    half = quarter // 2
    core = lax.axis_index("fsdp") % 2
    chip = lax.axis_index("dp")
    spot = jnp.stack([chip, core, 2 * core + chip % 2]).astype(jnp.int32)

    def matching(m, back):
        pairs = []
        for k in range(owners // 2):
            for c in range(2):
                for d in range(chips):
                    c2, j = (d ^ m) >> 1, (d ^ m) & 1
                    here = (2 * k + c) * chips + d
                    there = (2 * k + c2) * chips + 2 * c + j
                    pairs.append((there, here) if back else (here, there))
        return pairs

    swap = [(i, i ^ 1) for i in range(owners)]

    packed = pl.pallas_call(
        pack_kernel,
        out_shape=[shape((2 * half, order), BF16)] * chips,
        in_specs=[SMEM] + [pl.BlockSpec(memory_space=pl.ANY)] * 2,
        out_specs=[pl.BlockSpec(memory_space=pl.ANY)] * chips,
        scratch_shapes=[pltpu.SemaphoreType.DMA((chips * (1 + order // half),))],
        compiler_params=pltpu.CompilerParams(vmem_limit_bytes=60 * MIB),
        cost_estimate=pl.CostEstimate(flops=0, bytes_accessed=4 * MIB, transcendentals=0),
    )(spot, root_left, root_right)
    roots = [lax.ppermute(packed[m], AXES, matching(m, False)) for m in range(chips)]

    pieces = local(
        spread_kernel, shape((devices, piece_rows, half), BF16), (block_slot, gradient),
        scratch=[pltpu.VMEM((2 * blocks * piece_rows, half), F32)], limit=6, moved=MIB * 3 // 2,
    )

    def spread(x, slots, g, second):
        x = lax.all_to_all(x, AXES, split_axis=0, concat_axis=0, tiled=True)
        new, sums = local(
            moment_kernel,
            [shape(second.shape, F32), shape((devices, 1, 128), F32)],
            (slots, g, second),
            scratch=[pltpu.VMEM((blocks, 128), F32)], limit=6, moved=MIB * 5 // 2,
        )
        return x, new, sums

    own, new_second, sent = lax.cond(
        block_slot[0] >= 0,
        spread,
        lambda x, slots, g, second: (jnp.zeros_like(x), jnp.zeros_like(second), jnp.zeros((devices, 1, 128), F32)),
        pieces, block_slot, gradient, second_moment,
    )
    adam = lax.all_to_all(sent, AXES, split_axis=0, concat_axis=0, tiled=True)

    own, *roots = lax.optimization_barrier((own, *roots))
    left, right = local(
        unpack_kernel, [shape((order // 2, order), BF16), shape((chips, half, order), BF16)], (spot, *roots),
        limit=5, moved=4 * MIB,
    )
    left2 = lax.ppermute(left, "fsdp", swap)
    other = lax.ppermute(own, "fsdp", swap)

    cut = (owners, chips, piece_rows, half)
    grad, update, norm = local(
        update_kernel,
        [shape((order, order), BF16), shape(cut, BF16), shape((8, 128), F32)],
        (spot, own.reshape(cut), other.reshape(cut), left, left2, right),
        scratch=[pltpu.VMEM((order, order // 2), BF16)] * 2,
        flops=2 * order * order * order, limit=18, moved=8 * MIB,
    )
    norm2 = lax.ppermute(norm, "fsdp", swap)
    products = local(
        product_kernel, [shape((2 * half, order), BF16)] * chips, (spot, grad),
        scratch=[pltpu.VMEM((order // 2, order), BF16)] * 2,
        flops=2 * order * order * order, limit=11, moved=4 * MIB,
    )
    update, *products = lax.optimization_barrier((update, *products))
    back = local(graft_kernel, shape(cut, BF16), (spot, update, norm, norm2, adam), limit=5, moved=2 * MIB)
    products = [lax.ppermute(products[m], AXES, matching(m, True)) for m in range(chips)]
    returned = lax.all_to_all(back.reshape(devices, piece_rows, half), AXES, split_axis=0, concat_axis=0, tiled=True)

    anywhere = pl.BlockSpec(memory_space=pl.ANY)
    new_left, new_right = pl.pallas_call(
        stat_kernel,
        out_shape=[shape(stat_left.shape, F32), shape(stat_right.shape, F32)],
        in_specs=[SMEM] + [VMEM] * chips + [anywhere] * 2,
        out_specs=[anywhere] * 2,
        scratch_shapes=[pltpu.VMEM((2 * chips, half, order), F32), pltpu.SemaphoreType.DMA((2, 2 * chips))],
        compiler_params=pltpu.CompilerParams(vmem_limit_bytes=10 * MIB),
        cost_estimate=pl.CostEstimate(flops=0, bytes_accessed=10 * MIB, transcendentals=0),
    )(spot, *products, stat_left, stat_right)

    direction = local(
        direction_kernel, shape(gradient.shape, gradient.dtype), (block_slot, returned),
        scratch=[pltpu.VMEM((2 * blocks * piece_rows, half), F32)],
        limit=7, moved=2 * MIB,
    )
    return (new_left, new_right, new_second, direction)


def solution(mesh):
    placed = (
        P(None, "fsdp", None, "dp"),
        P(None, "fsdp", None, "dp"),
        P("fsdp", "dp", None),
        P("fsdp", "dp", None),
        P("fsdp", "dp", None),
        P("fsdp", None, "dp"),
        P(),
    )
    return jax.shard_map(
        body,
        mesh=mesh,
        in_specs=placed,
        out_specs=(
            P("fsdp", "dp", None),
            P("fsdp", "dp", None),
            P(None, "fsdp", None, "dp"),
            P(None, "fsdp", None, "dp"),
        ),
        check_vma=False,
    )
```
